512 devices in a mesh: row: 16 (over z, core), col: 32 (over y, x).
Axes of the slice: x: 4, y: 8, z: 8, core: 2. Of those that a mesh axis runs over, the one named last changes fastest.
Arguments:
- band_sites: float32 [2, 512], P(None, 'row'), may hold values from 0 to 1
- test_sites: float32 [2, 4096], P(None, 'col'), may hold values from 0 to 1
- band_factor: float32 [512, 512], P('row', 'col'), as said below
- prior_factor: float32 [512, 8192], P('row', 'col'), may hold values from -0.0625 to 0.0625
- prior_solution: float32 [8192, 4096], P('col', 'row'), may hold values from -6 to 6
- prior_covariance: float32 [4096, 4096], P('row', 'col'), may hold values from -4 to 4
Outputs:
- band_solution: float32 [512, 4096], P('row', 'col')
- covariance: float32 [4096, 4096], P('row', 'col')
The draws below stay inside these ranges and needn't reach their ends.
Inputs may be any that keep to these rules, and one draw needn't show every extreme that they name: band_factor is lower triangular with diagonal entries in 1 to 2 and small entries below it.
All inputs are finite; a program needn't handle non-finite values.
Results may differ from the reference program's by a relative error of at most 0.00011.
Values sent between devices are 32-bit elements; how exact they have to be, the bound alone decides.
A program may use at most 64 MiB of HBM per device.

```python
import jax
import jax.numpy as jnp
from jax import lax

BAND = 512
TESTS = 4096
PREV = 8192


def draw_band_factor(key, part):
    first_key = jax.random.fold_in(key, 11)
    second_key = jax.random.fold_in(key, 23)
    lower_part = jax.random.normal(first_key, (BAND, BAND), jnp.float32) * (0.5 / BAND ** 0.5)
    row_index = jnp.arange(BAND)[:, None]
    col_index = jnp.arange(BAND)[None, :]
    lower_part = jnp.where(row_index > col_index, lower_part, 0.0)
    diagonal = jax.random.uniform(second_key, (BAND,), jnp.float32, 1.0, 2.0)
    return lower_part + jnp.diag(diagonal)


def spiked(drawn, stream_key, source, target, parts, factor):
    def block_of(axis_at):
        return (jnp.arange(drawn.shape[axis_at]) // (drawn.shape[axis_at] // parts)).reshape((-1,) + (1,) * (drawn.ndim - 1 - axis_at))

    one_side = jax.random.permutation(stream_key, parts)[block_of(target)]
    second = (block_of(target) + parts // 2) % parts
    return jnp.where((block_of(source) == one_side) | (block_of(source) == second), factor * drawn, drawn)


def level_of(rng, shape, pieces, low, largest):
    def one(position, shards_of):
        heights = jax.random.uniform(jax.random.fold_in(jax.random.fold_in(rng, 6), position), (shards_of,), jnp.float32, low / len(pieces), largest / len(pieces))
        return jnp.repeat(jnp.exp(heights), shape[position] // shards_of).reshape((-1,) + (1,) * (len(shape) - position - 1))

    level = one(*pieces[0])
    for cut in pieces[1:]:
        level = level * one(*cut)
    return level


def normal_values(rng, extent, scale, limit, cuts=(), held_as=jnp.bfloat16):
    entries = jax.random.normal(rng, extent, jnp.float32) * scale
    if len(cuts) > 0:
        entries = level_of(rng, extent, cuts, -0.22, 0.18) * entries
    return jnp.clip(entries, min=-limit, max=limit).astype(held_as)


def bell_draw_with(own_key, dims, scale, limit, cuts, heavy, kind=jnp.bfloat16):
    drawn = scale * jax.random.normal(own_key, dims, jnp.float32)
    if cuts:
        drawn = drawn * level_of(own_key, dims, cuts, -0.22, 0.18)
    return jnp.clip(spiked(drawn, jax.random.fold_in(own_key, 3), *heavy), -limit, limit).astype(kind)


def setup_inputs(seed: int = 0) -> dict:
    streams_of = jax.random.split(jax.random.key(seed), 7)
    band_sites = jnp.clip(1.0 * jax.random.uniform(streams_of[0], (2, BAND), jnp.float32) ** level_of(streams_of[0], (2, BAND), ((1, 16),), -0.2, 0.2), 0.0, 1.0)
    test_sites = jnp.clip(1.0 * jax.random.uniform(streams_of[1], (2, TESTS), jnp.float32) ** level_of(streams_of[1], (2, TESTS), ((1, 32),), -0.2, 0.2), 0.0, 1.0)
    band_factor = draw_band_factor(jax.random.fold_in(streams_of[6], 71), 0)
    prior_factor = normal_values(streams_of[3], (BAND, PREV), PREV ** -0.5, 0.0625, ((0, 16), (1, 32)), jnp.float32)
    prior_solution = bell_draw_with(streams_of[4], (PREV, TESTS), 1.0, 6.0, ((0, 32), (1, 16)), (0, 1, 32, 2.75), jnp.float32)
    prior_covariance = normal_values(streams_of[5], (TESTS, TESTS), 0.5, 4.0, ((0, 16), (1, 32)), jnp.float32)
    return dict(band_sites=band_sites, test_sites=test_sites, band_factor=band_factor, prior_factor=prior_factor, prior_solution=prior_solution, prior_covariance=prior_covariance)


length_scale = 0.3

def matern(band_sites, test_sites):
    delta_x = band_sites[0][:, None] - test_sites[0][None, :]
    delta_y = band_sites[1][:, None] - test_sites[1][None, :]
    scaled = jnp.sqrt(delta_x * delta_x + delta_y * delta_y + 1e-06) * (3.0 ** 0.5 / length_scale)
    return (1.0 + scaled) * jnp.exp(-scaled)

def reference(band_sites, test_sites, band_factor, prior_factor, prior_solution, prior_covariance):
    cross = matern(band_sites, test_sites)
    update = jnp.dot(prior_factor.astype(jnp.float32), prior_solution.astype(jnp.float32), precision=lax.Precision.HIGHEST, preferred_element_type=jnp.float32)
    remaining = cross - update
    band_solution = lax.linalg.triangular_solve(band_factor, remaining, left_side=True, lower=True)
    gram_sum = lax.dot_general(band_solution.astype(jnp.float32), band_solution.astype(jnp.float32), (((0,), (0,)), ((), ())), precision=lax.Precision.HIGHEST, preferred_element_type=jnp.float32)
    return (band_solution, prior_covariance - gram_sum)
```

```python
import jax
import jax.numpy as jnp
from jax import lax
from jax.experimental import pallas as pl
from jax.experimental.pallas import tpu as pltpu
from jax.sharding import PartitionSpec as P

length_scale = 0.3
MESH = pl.DeviceIdType.MESH
F32 = jnp.float32
BF16 = jnp.bfloat16
NZ, NY, NX = 8, 8, 4


def halves(value):
    high = value.astype(BF16)
    return high, (value - high.astype(F32)).astype(BF16)


def dot(a, b, dims):
    return lax.dot_general(a, b, (dims, ((), ())), preferred_element_type=F32)


def dot3(a, b, dims=((1,), (0,))):
    (ah, al), (bh, bl) = a, b
    return dot(ah, bh, dims) + (dot(ah, bl, dims) + dot(al, bh, dims))


def mul(a, b):
    return dot3(halves(a), halves(b))


def upper_inverses(blocks):
    n = 128
    i = lax.broadcasted_iota(jnp.int32, (n, n), 0)
    j = lax.broadcasted_iota(jnp.int32, (n, n), 1)
    done = []
    for u in blocks:
        inv = jnp.where(i == j, 1.0 / jnp.where(i == j, u, 1.0), 0.0)
        down = jnp.sum(inv, axis=1, keepdims=True)
        across = jnp.sum(inv, axis=0, keepdims=True)
        pair = (i // 2 == j // 2) & (i < j)
        done.append(inv - jnp.where(pair, u * down * across, 0.0))
    size = 2
    while size < n:
        part = (i // (2 * size) == j // (2 * size)) & (i // size < j // size)
        left = [halves(x) for x in done]
        mid = [dot3(x, halves(jnp.where(part, u, 0.0))) for x, u in zip(left, blocks)]
        done = [x - dot3(halves(m), xh) for x, m, xh in zip(done, mid, left)]
        size *= 2
    return done


def kernel(
    bs, ts, lf, a, s, pc, v_out, cov_out,
    abuf, sh, sl, pb, xb, ys, yb, cr, sb,
    lzs, lz, lms, lp, lt16, lt, yi, wh, wl,
    own, rr, zb, rcx, rc,
    send, rec, a_rec, ap_rec,
):
    row = lax.axis_index("row")
    col = lax.axis_index("col")
    z, core = row // 2, row % 2
    y, x = col // NX, col % NX
    partner = (2 * z + 1 - core, col)

    def at_z(zz):
        return (2 * zz + core, col)

    def at_y(yy):
        return (row, yy * NX + x)

    def at_x(xx):
        return (row, y * NX + xx)

    def push(src, dst, k, device, recv=None):
        pltpu.make_async_remote_copy(
            src_ref=src,
            dst_ref=dst,
            send_sem=send.at[k],
            recv_sem=rec.at[k] if recv is None else recv,
            device_id=device,
            device_id_type=MESH,
        ).start()

    def await_bytes(ref, sem):
        pltpu.make_async_copy(ref, ref, sem).wait()

    barrier = pltpu.get_barrier_semaphore()
    peers = [partner]
    peers += [at_z((z + d) % NZ) for d in range(1, NZ)]
    peers += [at_y((y + d) % NY) for d in range(1, NY)]
    peers += [at_x((x + d) % NX) for d in range(1, NX)]
    for peer in peers:
        pl.semaphore_signal(barrier, inc=1, device_id=peer, device_id_type=MESH)
    pl.semaphore_wait(barrier, len(peers))

    k_lz, k_lp, k_ly1, k_ly0, k_lx1, k_lx0, k_lq1, k_lq0, k_yi = range(9)
    k_a, k_ap, k_sz, k_sp, k_px, k_uy, k_ry, k_rz, k_cy, k_rx, k_cx, k_cp = range(9, 21)

    place = (
        lax.broadcasted_iota(jnp.int32, (32, 128), 1)
        == lax.broadcasted_iota(jnp.int32, (32, 128), 0) + 32 * (row % 4)
    ).astype(F32)
    tile = lax.dot_general(
        lf[...], place, (((0,), (0,)), ((), ())),
        precision=lax.Precision.HIGHEST, preferred_element_type=F32,
    )
    lzs[...] = tile
    lz[z] = tile
    for d in range(1, NZ):
        push(lzs, lz.at[z], k_lz, at_z((z + d) % NZ))
    push(a, abuf.at[z, core], k_ap, partner, ap_rec.at[z])
    for d in (1, 7, 2, 6, 3, 5, 4):
        push(a, abuf.at[z, core], k_a, at_z((z + d) % NZ), a_rec.at[z])
    abuf[z, core] = a[...]
    sb[z, core, 0:2, 0:32] = bs[...]

    @pl.when(z != y)
    def _():
        push(sb.at[z, core], sb.at[z, core], k_sz, at_z(y))

    sh[...], sl[...] = halves(s[...])

    await_bytes(lz.at[0:7], rec.at[k_lz])
    for q in range(4):
        lms[q] = lz[2 * q] + lz[2 * q + 1]
    push(lms, lp, k_lp, partner)

    root_core = x // 2

    @pl.when(z == y)
    def _():
        await_bytes(sb.at[0:7, 0], rec.at[k_sz])

        @pl.when(core != root_core)
        def _():
            push(sb.at[:, core], sb.at[:, core], k_sp, partner)

    await_bytes(lp, rec.at[k_lp])
    for q in range(4):
        lt16[q] = lms[q] + lp[q]
    lt[core, 0, y, x] = lt16[core]
    lt[core, 1, y, x] = lt16[3 - core]
    for d in range(1, NY):
        push(lt.at[core, 1, y, x], lt.at[core, 1, y, x], k_ly1, at_y((y + d) % NY))

    @pl.when(y < 4)
    def _():
        for d in range(1, NY):
            push(lt.at[core, 0, y, x], lt.at[core, 0, y, x], k_ly0, at_y((y + d) % NY))

    root = (z == y) & (core == root_core)

    @pl.when(root)
    def _():
        await_bytes(sb.at[:, 0], rec.at[k_sp])
        tx, ty = ts[0:1, :], ts[1:2, :]
        for zz in range(NZ):
            for cc in range(2):
                spots = sb[zz, cc].T
                dx = spots[0:32, 0:1] - tx
                dy = spots[0:32, 1:2] - ty
                scaled = jnp.sqrt(dx * dx + dy * dy + 1e-06) * (3.0**0.5 / length_scale)
                cr[zz, cc] = (1.0 + scaled) * jnp.exp(-scaled)

    pair0 = z // 2
    for step, o in enumerate((0, 1, 3, 2)):
        p = (pair0 + o) % 4
        for zz in (2 * p, 2 * p + 1):

            @pl.when(zz != z)
            def _():
                await_bytes(a, a_rec.at[zz])
                push(abuf.at[zz, core], abuf.at[zz, core], k_ap, partner, ap_rec.at[zz])

        for zz in (2 * p, 2 * p + 1):
            await_bytes(a, ap_rec.at[zz])
        rows = abuf[pl.ds(2 * p, 2)].reshape(128, 256)
        pb[p] = dot3(halves(rows), (sh[...], sl[...]))

        @pl.when(root)
        def _():
            lanes = pl.ds(pl.multiple_of(128 * (x % 2), 128), 128)
            pb[p, :, lanes] = pb[p, :, lanes] - cr[pl.ds(2 * p, 2)].reshape(128, 128)

        @pl.when(p != x)
        def _():
            push(pb.at[p], xb.at[x], k_px, at_x(p))

        if step == 1:
            await_bytes(lt.at[0, 1, 0:7, 0], rec.at[k_ly1])

            @pl.when(y < 4)
            def _():
                await_bytes(lt.at[0, 0, 0:3, 0], rec.at[k_ly0])

            @pl.when(y >= 4)
            def _():
                await_bytes(lt.at[0, 0, 0:4, 0], rec.at[k_ly0])

            for d in range(1, NX):
                push(lt.at[core, 1, :, x], lt.at[core, 1, :, x], k_lx1, at_x((x + d) % NX))
                push(lt.at[core, 0, 0:4, x], lt.at[core, 0, 0:4, x], k_lx0, at_x((x + d) % NX))

    xb[x] = pb[x]
    await_bytes(lt.at[0, 1, :, 0:3], rec.at[k_lx1])
    await_bytes(lt.at[0, 0, 0:4, 0:3], rec.at[k_lx0])
    push(lt.at[core, 1], lt.at[core, 1], k_lq1, partner)
    push(lt.at[core, 0, 0:4], lt.at[core, 0, 0:4], k_lq0, partner)

    await_bytes(xb.at[0:3], rec.at[k_px])
    total = (xb[0] + xb[1]) + (xb[2] + xb[3])
    ys[...] = total.reshape(8, 16, 256)
    for d in range(1, NY):
        push(ys.at[(y + d) % NY], yb.at[y], k_uy, at_y((y + d) % NY))
    yb[y] = ys[y]

    q0, q1 = core, 3 - core
    u0 = lt[core, 0, pl.ds(2 * q0, 2)].reshape(128, 128)
    u1 = lt[core, 1, pl.ds(2 * q1, 2)].reshape(128, 128)
    w0, w1 = upper_inverses([u0, u1])
    yi[q0] = w0
    yi[q1] = w1
    push(yi.at[q0], yi.at[q0], k_yi, partner)
    push(yi.at[q1], yi.at[q1], k_yi, partner)

    await_bytes(yb.at[0:7], rec.at[k_uy])
    mine = -(((yb[0] + yb[1]) + (yb[2] + yb[3])) + ((yb[4] + yb[5]) + (yb[6] + yb[7])))
    own[...] = mine
    for d in range(1, NZ):
        push(own, zb.at[z], k_rz, at_z((z + d) % NZ))
    for d in range(1, NY):
        push(own, rr.at[x, y], k_ry, at_y((y + d) % NY))
    zb[z] = mine
    rr[x, y] = mine
    await_bytes(zb.at[0:7], rec.at[k_rz])
    for d in range(1, NY):
        push(zb.at[(y + d) % NY], rcx.at[y], k_cy, at_y((y + d) % NY))
    rcx[y] = zb[y]
    await_bytes(rr.at[0, 0:7], rec.at[k_ry])
    for d in range(1, NX):
        push(rr.at[x], rr.at[x], k_rx, at_x((x + d) % NX))
    await_bytes(rcx.at[0:7], rec.at[k_cy])
    mine_here = root_core == core
    for half in range(2):
        xx = 2 * core + half
        lanes = slice(128 * half, 128 * half + 128)

        @pl.when(xx != x)
        def _():
            push(rcx.at[:, :, lanes], rc.at[x], k_cx, at_x(xx))

        @pl.when(xx == x)
        def _():
            rc[x] = rcx[:, :, lanes]

    await_bytes(yi.at[0:2], rec.at[k_yi])
    await_bytes(lt.at[0, 1], rec.at[k_lq1])
    await_bytes(lt.at[0, 0, 0:4], rec.at[k_lq0])
    where = {0: (0, 0), 3: (0, 1), 1: (1, 0), 2: (1, 1)}

    def block(j, q):
        k, slot = where[q]
        return halves(lt[k, slot, 2 * j : 2 * j + 2].reshape(128, 128))

    w = [yi[q] for q in range(4)]
    ws = [halves(v) for v in w]
    w01 = -dot3(halves(dot3(ws[0], block(0, 1))), ws[1])
    w23 = -dot3(halves(dot3(ws[2], block(2, 3))), ws[3])
    h01, h23 = halves(w01), halves(w23)
    t02 = halves(dot3(ws[0], block(0, 2)) + dot3(h01, block(1, 2)))
    t03 = halves(dot3(ws[0], block(0, 3)) + dot3(h01, block(1, 3)))
    t12 = halves(dot3(ws[1], block(1, 2)))
    t13 = halves(dot3(ws[1], block(1, 3)))
    w02 = -dot3(t02, ws[2])
    w03 = -(dot3(t02, h23) + dot3(t03, ws[3]))
    w12 = -dot3(t12, ws[2])
    w13 = -(dot3(t12, h23) + dot3(t13, ws[3]))
    full = {(0, 0): w[0], (1, 1): w[1], (2, 2): w[2], (3, 3): w[3]}
    full.update({(0, 1): w01, (2, 3): w23, (0, 2): w02, (0, 3): w03, (1, 2): w12, (1, 3): w13})
    for j in range(4):
        for q in range(4):
            here = (slice(128 * q, 128 * q + 128), slice(128 * j, 128 * j + 128))
            if (j, q) in full:
                wh[here], wl[here] = halves(full[j, q].T)
            else:
                wh[here] = jnp.zeros((128, 128), BF16)
                wl[here] = jnp.zeros((128, 128), BF16)

    await_bytes(rr.at[0:3], rec.at[k_rx])
    inverse = (wh[...], wl[...])
    vr = dot3(inverse, halves(rr[...].reshape(512, 256)))

    @pl.when(mine_here)
    def _():
        await_bytes(rc.at[0:3], rec.at[k_cx])
        push(rc, rc, k_cp, partner)

    @pl.when(root_core != core)
    def _():
        await_bytes(rc, rec.at[k_cp])

    vc = dot3(inverse, halves(rc[...].reshape(512, 128)))
    rc_rows = vc.reshape(16, 32, 128)
    cov_out[...] = pc[...] - dot3(halves(vr), halves(vc), ((0,), (0,)))
    xb[0, :, 0:128] = rc_rows[0:4].reshape(128, 128)
    xb[1, :, 0:128] = rc_rows[4:8].reshape(128, 128)
    xb[2, :, 0:128] = rc_rows[8:12].reshape(128, 128)
    xb[3, :, 0:128] = rc_rows[12:16].reshape(128, 128)
    v_out[...] = xb[row // 4, pl.ds(pl.multiple_of(32 * (row % 4), 32), 32), 0:128]

    await_bytes(lz.at[0:7], send.at[k_lz])
    await_bytes(lp, send.at[k_lp])
    await_bytes(lt.at[0, 1, 0:7, 0], send.at[k_ly1])

    @pl.when(y < 4)
    def _():
        await_bytes(lt.at[0, 0, 0:7, 0], send.at[k_ly0])

    await_bytes(lt.at[0, 1, :, 0:3], send.at[k_lx1])
    await_bytes(lt.at[0, 0, 0:4, 0:3], send.at[k_lx0])
    await_bytes(lt.at[0, 1], send.at[k_lq1])
    await_bytes(lt.at[0, 0, 0:4], send.at[k_lq0])
    await_bytes(yi.at[0:2], send.at[k_yi])
    await_bytes(abuf.at[0:7, 0], send.at[k_a])
    await_bytes(abuf.at[:, 0], send.at[k_ap])

    @pl.when(z != y)
    def _():
        await_bytes(sb.at[0, 0], send.at[k_sz])

    @pl.when((z == y) & (core != root_core))
    def _():
        await_bytes(sb.at[:, 0], send.at[k_sp])

    await_bytes(xb.at[0:3], send.at[k_px])
    await_bytes(yb.at[0:7], send.at[k_uy])
    await_bytes(zb.at[0:7], send.at[k_rz])
    await_bytes(rr.at[0, 0:7], send.at[k_ry])
    await_bytes(rcx.at[0:7], send.at[k_cy])
    await_bytes(rr.at[0:3], send.at[k_rx])

    @pl.when(mine_here)
    def _():
        await_bytes(rc.at[0], send.at[k_cx])
        await_bytes(rc, send.at[k_cp])

    @pl.when(root_core != core)
    def _():
        await_bytes(rc.at[0:2], send.at[k_cx])


def local(band_sites, test_sites, band_factor, prior_factor, prior_solution, prior_covariance):
    vmem = pl.BlockSpec(memory_space=pltpu.VMEM)
    scratch = [
        pltpu.VMEM((8, 2, 32, 256), F32),
        pltpu.VMEM((256, 256), BF16),
        pltpu.VMEM((256, 256), BF16),
        pltpu.VMEM((4, 128, 256), F32),
        pltpu.VMEM((4, 128, 256), F32),
        pltpu.VMEM((8, 16, 256), F32),
        pltpu.VMEM((8, 16, 256), F32),
        pltpu.VMEM((8, 2, 32, 128), F32),
        pltpu.VMEM((8, 2, 8, 128), F32),
        pltpu.VMEM((16, 128), F32),
        pltpu.VMEM((8, 16, 128), F32),
        pltpu.VMEM((4, 16, 128), F32),
        pltpu.VMEM((4, 16, 128), F32),
        pltpu.VMEM((4, 16, 128), F32),
        pltpu.VMEM((2, 2, 8, 4, 16, 128), F32),
        pltpu.VMEM((4, 128, 128), F32),
        pltpu.VMEM((512, 512), BF16),
        pltpu.VMEM((512, 512), BF16),
        pltpu.VMEM((16, 256), F32),
        pltpu.VMEM((4, 8, 16, 256), F32),
        pltpu.VMEM((8, 16, 256), F32),
        pltpu.VMEM((8, 16, 256), F32),
        pltpu.VMEM((4, 8, 16, 128), F32),
        pltpu.SemaphoreType.DMA((21,)),
        pltpu.SemaphoreType.DMA((21,)),
        pltpu.SemaphoreType.DMA((8,)),
        pltpu.SemaphoreType.DMA((8,)),
    ]
    return pl.pallas_call(
        kernel,
        out_shape=(
            jax.ShapeDtypeStruct((32, 128), F32),
            jax.ShapeDtypeStruct((256, 128), F32),
        ),
        in_specs=[vmem] * 6,
        out_specs=(vmem, vmem),
        scratch_shapes=scratch,
        compiler_params=pltpu.CompilerParams(
            collective_id=0, has_side_effects=True, vmem_limit_bytes=32 * 1024 * 1024
        ),
    )(band_sites, test_sites, band_factor, prior_factor, prior_solution, prior_covariance)


def solution(mesh):
    placed = (
        P(None, "row"),
        P(None, "col"),
        P("row", "col"),
        P("row", "col"),
        P("col", "row"),
        P("row", "col"),
    )
    return jax.shard_map(
        local,
        mesh=mesh,
        in_specs=placed,
        out_specs=(P("row", "col"), P("row", "col")),
        check_vma=False,
    )
```

```python
import jax
import jax.numpy as jnp
from jax import lax
from jax.experimental import pallas as pl
from jax.experimental.pallas import tpu as pltpu
from jax.sharding import PartitionSpec as P

length_scale = 0.3
MESH = pl.DeviceIdType.MESH
F32 = jnp.float32
BF16 = jnp.bfloat16
NZ, NY, NX = 8, 8, 4


def halves(value):
    high = value.astype(BF16)
    return high, (value - high.astype(F32)).astype(BF16)


def dot(a, b, dims):
    return lax.dot_general(a, b, (dims, ((), ())), preferred_element_type=F32)


def dot3(a, b, dims=((1,), (0,))):
    (ah, al), (bh, bl) = a, b
    return dot(ah, bh, dims) + (dot(ah, bl, dims) + dot(al, bh, dims))


def upper_inverses(blocks):
    n = 128
    i = lax.broadcasted_iota(jnp.int32, (n, n), 0)
    j = lax.broadcasted_iota(jnp.int32, (n, n), 1)
    done = []
    for u in blocks:
        inv = jnp.where(i == j, 1.0 / jnp.where(i == j, u, 1.0), 0.0)
        down = jnp.sum(inv, axis=1, keepdims=True)
        across = jnp.sum(inv, axis=0, keepdims=True)
        pair = (i // 2 == j // 2) & (i < j)
        done.append(inv - jnp.where(pair, u * down * across, 0.0))
    size = 2
    while size < n:
        part = (i // (2 * size) == j // (2 * size)) & (i // size < j // size)
        left = [halves(x) for x in done]
        mid = [dot3(x, halves(jnp.where(part, u, 0.0))) for x, u in zip(left, blocks)]
        done = [x - dot3(halves(m), xh) for x, m, xh in zip(done, mid, left)]
        size *= 2
    return done


def placed_at(value, offset):
    at = lax.broadcasted_iota(jnp.int32, (32, 128), 1)
    it = lax.broadcasted_iota(jnp.int32, (32, 128), 0)
    return lax.dot_general(
        value, (at == it + offset).astype(F32), (((1,), (0,)), ((), ())),
        precision=lax.Precision.HIGHEST, preferred_element_type=F32,
    )


NAMES = (
    "lz", "bz", "lp", "bp", "ly0", "ly1", "lx0", "lx1", "lq0", "lq1", "w",
    "a", "ap", "ts", "rx", "cy", "cp", "ux", "uy", "ry", "rz",
)
K = {name: k for k, name in enumerate(NAMES)}
LOADS = ("lf", "bs", "a", "ts", "s", "pc")
TAKING = ((2, 8), (4, 6))
BLOCKS = [(j, q) for j in range(4) for q in range(j, 4)]
NEAR_FIRST = (1, 7, 2, 6, 3, 5, 4)
FAR_FIRST = (4, 3, 5, 2, 6, 1, 7)


def order_of(zz):
    turn = 2 * (zz % 2) - 1
    return [(zz // 2 + o) % 4 for o in (0, 4 + turn, 4 - turn, 2)]


def kernel(
    bs_in, ts_in, lf_in, a_in, s_in, pc_in, v_out, cov_out,
    bs, ts, lf, a, s, pc,
    abuf, sh, sl, pb, xb, xs, ub, tsb, tsr, lps, lzo, lzp, lt16, lt, wf, wh, wl,
    cr, own, rr, zb, rc, vs,
    load, send, rec, a_rec, ap_rec, ux_rec, uy_rec, ry_rec, rz_rec,
):
    row = lax.axis_index("row")
    col = lax.axis_index("col")
    z, core = row // 2, row % 2
    y, x = col // NX, col % NX
    partner = (2 * z + 1 - core, col)
    takes = core == x // 2
    rests = core != x // 2
    half = x % 2
    order = order_of(z)

    def at_z(zz):
        return (2 * zz + core, col)

    def at_y(yy):
        return (row, yy * NX + x)

    def at_x(xx):
        return (row, y * NX + xx)

    def push(src, dst, name, device, recv=None):
        pltpu.make_async_remote_copy(
            src_ref=src,
            dst_ref=dst,
            send_sem=send.at[K[name]],
            recv_sem=rec.at[K[name]] if recv is None else recv,
            device_id=device,
            device_id_type=MESH,
        ).start()

    def await_bytes(ref, sem):
        pltpu.make_async_copy(ref, ref, sem).wait()

    with jax.named_scope("signals"):
        barrier = pltpu.get_barrier_semaphore()
        peers = []
        for d in FAR_FIRST:
            peers += [at_z((z + d) % NZ), at_y((y + d) % NY)]
        peers += [at_x((x + d) % NX) for d in (2, 1, 3)] + [partner]
        for peer in peers:
            pl.semaphore_signal(barrier, inc=1, device_id=peer, device_id_type=MESH)
    into = dict(lf=(lf_in, lf), bs=(bs_in, bs), a=(a_in, a), ts=(ts_in, ts), s=(s_in, s), pc=(pc_in, pc))
    loads = {n: pltpu.make_async_copy(*into[n], load.at[k]) for k, n in enumerate(LOADS)}
    for n in LOADS:
        loads[n].start()

    with jax.named_scope("prepare"):
        loads["lf"].wait()
        lps[0] = placed_at(lf[0:8], 32 * core) + placed_at(lf[8:16], 64 + 32 * core)
        loads["bs"].wait()
        lps[1] = jnp.zeros((8, 128), F32)
        lps[1, 0:2] = placed_at(bs[...], 32 * (row % 4))
        loads["a"].wait()

    with jax.named_scope("barrier"):
        pl.semaphore_wait(barrier, len(peers))

    root = takes & (y == z)
    with jax.named_scope("first_sends"):
        for d in FAR_FIRST:
            push(lps.at[0], lzo.at[0, z], "lz", at_z((z + d) % NZ))
        push(a, abuf.at[z, core], "ap", partner, ap_rec.at[z])
        for d in NEAR_FIRST:
            push(a, abuf.at[z, core], "a", at_z((z + d) % NZ), a_rec.at[z])
        for d in FAR_FIRST:
            push(lps.at[1], lzo.at[1, z], "bz", at_z((z + d) % NZ))
        abuf[z, core] = a[...]
        lzo[:, z] = lps[...]
        loads["ts"].wait()

        @pl.when(root)
        def _():
            for k in range(2):
                tsb[:, k] = jnp.broadcast_to(ts[k : k + 1], (128, 128)).T.reshape(NY, 16, 128)
            for d in FAR_FIRST:
                yy = (y + d) % NY
                push(tsb.at[yy], tsr, "ts", at_y(yy))
            tsr[...] = tsb[y]

        loads["s"].wait()
        sh[...], sl[...] = halves(s[...].T)

    def pass_on(o):
        with jax.named_scope("pass_on"):
            for zz in (2 * order[o], 2 * order[o] + 1):

                @pl.when(zz != z)
                def _():
                    await_bytes(a, a_rec.at[zz])
                    push(abuf.at[zz, core], abuf.at[zz, core], "ap", partner, ap_rec.at[zz])

    def product(o):
        p = order[o]
        with jax.named_scope("a_wait"):
            for zz in (2 * p, 2 * p + 1):
                await_bytes(a, ap_rec.at[zz])
        with jax.named_scope("product"):
            rows = abuf[pl.ds(2 * p, 2)].reshape(128, 256)
            out = dot3((sh[...], sl[...]), halves(rows), ((1,), (1,)))
            pb[o] = out.reshape(2, NY, 16, 128)
            for h in range(2):
                xx = 2 * core + h

                @pl.when(xx != x)
                def _():
                    push(pb.at[o, h], xb.at[o, x], "ux", at_x(xx), ux_rec.at[o])

                @pl.when(xx == x)
                def _():
                    xb[o, x] = pb[o, h]

    def x_sum(o):
        with jax.named_scope("x_wait"):
            await_bytes(xb.at[o, 0:3], ux_rec.at[o])
        with jax.named_scope("x_sum"):
            xs[o] = (xb[o, 0] + xb[o, 1]) + (xb[o, 2] + xb[o, 3])
            for d in FAR_FIRST:
                yy = (y + d) % NY
                push(xs.at[o, yy], ub.at[o, y], "uy", at_y(yy), uy_rec.at[o])
            ub[o, y] = xs[o, y]

    def cross():
        with jax.named_scope("cross"):

            @pl.when(y != z)
            def _():
                await_bytes(tsr, rec.at[K["ts"]])

            await_bytes(lzp.at[1], rec.at[K["bp"]])
            for p in range(4):
                spots = (lzo[1, 2 * p] + lzp[1, 2 * p]) + (lzo[1, 2 * p + 1] + lzp[1, 2 * p + 1])
                dx = tsr[0] - spots[0:1]
                dy = tsr[1] - spots[1:2]
                scaled = jnp.sqrt(dx * dx + dy * dy + 1e-06) * (3.0**0.5 / length_scale)
                cr[p] = (1.0 + scaled) * jnp.exp(-scaled)

    def y_sum(o):
        with jax.named_scope("y_wait"):
            await_bytes(ub.at[o, 0:7], uy_rec.at[o])
        with jax.named_scope("y_sum"):
            p = order[o]
            terms = [ub[o, k] for k in range(NY)]
            while len(terms) > 1:
                terms = [terms[i] + terms[i + 1] for i in range(0, len(terms), 2)]
            value = cr[p] - terms[0]
            own[o] = value
            for d in FAR_FIRST:
                push(own.at[o], zb.at[o, z], "rz", at_z((z + d) % NZ), rz_rec.at[o])
            for d in FAR_FIRST:
                push(own.at[o], rr.at[p, half, y], "ry", at_y((y + d) % NY), ry_rec.at[o])
            rr[p, half, y] = value
            zb[o, z] = value

    def forward(o):
        with jax.named_scope("z_wait"):
            await_bytes(zb.at[0, 0:7], rz_rec.at[o])
        with jax.named_scope("to_column"):
            for zz in range(NZ):
                p = order_of(zz)[o]

                @pl.when(zz != y)
                def _():
                    push(zb.at[o, zz], rc.at[p, y], "cy", at_y(zz))

                @pl.when(zz == y)
                def _():
                    rc[p, y] = zb[o, zz]

        with jax.named_scope("r_wait"):
            await_bytes(rr.at[0, 0, 0:7], ry_rec.at[o])
        with jax.named_scope("to_row"):
            for d in (2, 1, 3):
                there = rr.at[order[o], half]
                push(there, there, "rx", at_x((x + d) % NX))

    first_taking = 2 + 2 * core
    second_taking = 8 - 2 * core
    first_in = y < first_taking
    second_in = y < second_taking

    def await_some(slot, count, options, name):
        for n in options:

            @pl.when(count == n)
            def _():
                await_bytes(lt.at[0, slot, 0:n, 0], rec.at[K[name]])

    def factor_z():
        with jax.named_scope("factor_z"):
            await_bytes(lzo.at[0, 0:7], rec.at[K["lz"]])
            push(lzo.at[0], lzp.at[0], "lp", partner)

    def sites_z():
        with jax.named_scope("sites_z"):
            await_bytes(lzo.at[1, 0:7], rec.at[K["bz"]])
            push(lzo.at[1], lzp.at[1], "bp", partner)

    def factor_y():
        with jax.named_scope("factor_y"):
            await_bytes(lzp.at[0], rec.at[K["lp"]])
            low = lax.broadcasted_iota(jnp.int32, (8, 128), 1) < 64
            for q in range(4):
                t0, t1 = (lzo[0, k] + lzp[0, k] for k in (2 * q, 2 * q + 1))
                lt16[q, 0:8] = jnp.where(low, t0, pltpu.roll(t1, 64, 1))
                lt16[q, 8:16] = jnp.where(low, pltpu.roll(t0, 64, 1), t1)
            lt[core, 0, y, x] = lt16[core]
            lt[core, 1, y, x] = lt16[3 - core]

            def along_y(slot):
                here = lt.at[core, slot, y, x]
                for d in FAR_FIRST:
                    push(here, here, f"ly{slot}", at_y((y + d) % NY))

            pl.when(first_in)(lambda: along_y(0))
            pl.when(second_in)(lambda: along_y(1))

    def each_part(body):
        for k in range(2):

            @pl.when(core == k)
            def _():
                for slot in range(2):
                    body(k, slot, TAKING[k][slot])

    def factor_x():
        with jax.named_scope("factor_x"):
            await_some(0, first_taking - first_in.astype(jnp.int32), (1, 2, 3, 4), "ly0")
            await_some(1, second_taking - second_in.astype(jnp.int32), (5, 6, 7), "ly1")

            def along_x(k, slot, n):
                part = lt.at[k, slot, 0:n, x]
                for d in (2, 1, 3):
                    push(part, part, f"lx{slot}", at_x((x + d) % NX))

            each_part(along_x)

    def factor_arrives():
        with jax.named_scope("factor_arrives"):
            each_part(lambda k, slot, n: await_bytes(lt.at[k, slot, 0:n, 0:3], rec.at[K[f"lx{slot}"]]))

    def factor_pair():
        with jax.named_scope("factor_pair"):

            def across(k, slot, n):
                part = lt.at[k, slot, 0:n]
                push(part, part, f"lq{slot}", partner)

            each_part(across)

    def inverse():
        where = {0: (0, 0), 3: (0, 1), 1: (1, 0), 2: (1, 1)}

        def tile(j, q):
            k, slot = where[q]
            return lt[k, slot, 2 * j : 2 * j + 2].reshape(128, 128)

        def block(j, q):
            return halves(tile(j, q))

        with jax.named_scope("pair_wait"):
            for k in range(2):

                @pl.when(core == 1 - k)
                def _():
                    for slot in range(2):
                        await_bytes(lt.at[k, slot, 0 : TAKING[k][slot]], rec.at[K[f"lq{slot}"]])

        with jax.named_scope("inverse"):
            w = upper_inverses([tile(q, q) for q in range(4)])
            ws = [halves(v) for v in w]
            w01 = -dot3(halves(dot3(ws[0], block(0, 1))), ws[1])
            w23 = -dot3(halves(dot3(ws[2], block(2, 3))), ws[3])
            h01, h23 = halves(w01), halves(w23)
            t02 = halves(dot3(ws[0], block(0, 2)) + dot3(h01, block(1, 2)))
            t03 = halves(dot3(ws[0], block(0, 3)) + dot3(h01, block(1, 3)))
            t12 = halves(dot3(ws[1], block(1, 2)))
            t13 = halves(dot3(ws[1], block(1, 3)))
            w02 = -dot3(t02, ws[2])
            w03 = -(dot3(t02, h23) + dot3(t03, ws[3]))
            w12 = -dot3(t12, ws[2])
            w13 = -(dot3(t12, h23) + dot3(t13, ws[3]))
            full = {(0, 0): w[0], (1, 1): w[1], (2, 2): w[2], (3, 3): w[3]}
            full.update({(0, 1): w01, (2, 3): w23, (0, 2): w02, (0, 3): w03, (1, 2): w12, (1, 3): w13})
            for k, at in enumerate(BLOCKS):
                wf[k] = full[at]
            push(wf, wf, "w", partner)

    def split_inverse():
        with jax.named_scope("split"):
            for k, (j, q) in enumerate(BLOCKS):
                here = (slice(128 * j, 128 * j + 128), slice(128 * q, 128 * q + 128))
                wh[here], wl[here] = halves(wf[k])

    with jax.named_scope("zeros"):
        for j in range(1, 4):
            for ref in (wh, wl):
                ref[128 * j : 128 * j + 128, 0 : 128 * j] = jnp.zeros((128, 128 * j), BF16)

    pass_on(0)
    pass_on(1)
    product(0)
    factor_z()
    pass_on(2)
    product(1)
    factor_y()
    pass_on(3)
    product(2)
    sites_z()
    product(3)

    @pl.when(takes)
    def _():
        x_sum(0)
        x_sum(1)
        cross()
        x_sum(2)
        x_sum(3)
        factor_x()
        for o in range(4):
            y_sum(o)
        forward(0)
        factor_arrives()
        factor_pair()
        forward(1)
        forward(2)
        forward(3)
        with jax.named_scope("inverse_wait"):
            await_bytes(wf, rec.at[K["w"]])

    @pl.when(rests)
    def _():
        factor_x()
        factor_arrives()
        inverse()

    split_inverse()

    with jax.named_scope("column_wait"):

        @pl.when(takes)
        def _():
            await_bytes(rc.at[:, 0:7], rec.at[K["cy"]])
            push(rc, rc, "cp", partner)

    with jax.named_scope("row_wait"):

        @pl.when(takes)
        def _():
            await_bytes(rr.at[:, 0], rec.at[K["rx"]])

        @pl.when(rests)
        def _():
            await_bytes(rr, rec.at[K["rx"]])

    with jax.named_scope("row_solve"):
        solver = (wh[...], wl[...])
        right = jnp.concatenate([rr[p].reshape(256, 128) for p in range(4)], axis=1)
        vr = halves(dot3(halves(right), solver))
        loads["pc"].wait()
    with jax.named_scope("column_pair"):

        @pl.when(rests)
        def _():
            await_bytes(rc, rec.at[K["cp"]])
            await_bytes(lzp.at[1], rec.at[K["bp"]])

    with jax.named_scope("update"):
        right = jnp.concatenate([rc[p].reshape(128, 128) for p in range(4)], axis=1)
        vc = dot3(halves(right), solver)
        cov_out[...] = pc[...] - dot3(vr, halves(vc), ((1,), (1,)))
        for p in range(4):
            vs[p] = vc[:, 128 * p : 128 * p + 128]
        vs[4] = vs[row // 4].T
        v_out[...] = vs[4, pl.ds(pl.multiple_of(32 * (row % 4), 32), 32)]

    with jax.named_scope("drain"):
        await_bytes(lzo.at[0, 0:7], send.at[K["lz"]])
        await_bytes(lzo.at[1, 0:7], send.at[K["bz"]])
        await_bytes(lzo.at[0], send.at[K["lp"]])
        await_bytes(lzo.at[1], send.at[K["bp"]])
        pl.when(first_in)(lambda: await_bytes(lt.at[0, 0, 0:7, 0], send.at[K["ly0"]]))
        pl.when(second_in)(lambda: await_bytes(lt.at[0, 1, 0:7, 0], send.at[K["ly1"]]))
        each_part(lambda k, slot, n: await_bytes(lt.at[k, slot, 0:n, 0:3], send.at[K[f"lx{slot}"]]))
        await_bytes(abuf.at[0:7, 0], send.at[K["a"]])
        await_bytes(abuf.at[:, 0], send.at[K["ap"]])

        @pl.when(root)
        def _():
            await_bytes(tsb.at[0:7], send.at[K["ts"]])

        @pl.when(takes)
        def _():
            each_part(lambda k, slot, n: await_bytes(lt.at[k, slot, 0:n], send.at[K[f"lq{slot}"]]))
            await_bytes(xb.at[:, 0], send.at[K["ux"]])
            await_bytes(ub.at[:, 0:7], send.at[K["uy"]])
            await_bytes(zb.at[:, 0:7], send.at[K["rz"]])
            await_bytes(zb.at[:, 0:7], send.at[K["ry"]])
            await_bytes(xb.at[:, 0:3], send.at[K["rx"]])
            await_bytes(rc.at[:, 0:7], send.at[K["cy"]])
            await_bytes(rc, send.at[K["cp"]])

        @pl.when(rests)
        def _():
            await_bytes(xb.at[:, 0:2], send.at[K["ux"]])
            await_bytes(wf, send.at[K["w"]])


def local(band_sites, test_sites, band_factor, prior_factor, prior_solution, prior_covariance):
    vmem = pl.BlockSpec(memory_space=pltpu.VMEM)
    hbm = pl.BlockSpec(memory_space=pltpu.HBM)
    arrays = [
        (2, 32), (2, 128), (16, 32), (32, 256), (256, 256), (256, 128),
        (8, 2, 32, 256),
        BF16, BF16,
        (4, 2, NY, 16, 128),
        (4, NX, NY, 16, 128),
        (4, NY, 16, 128),
        (4, NY, 16, 128),
        (NY, 2, 16, 128),
        (2, 16, 128),
        (2, 8, 128),
        (2, 8, 8, 128), (2, 8, 8, 128),
        (4, 16, 128),
        (2, 2, 8, 4, 16, 128),
        (10, 128, 128),
        None, None,
        (4, 16, 128), (4, 16, 128),
        (4, 2, NY, 16, 128),
        (4, NZ, 16, 128),
        (4, NY, 16, 128),
        (5, 128, 128),
    ]
    scratch = []
    for shape in arrays:
        if shape is BF16:
            scratch.append(pltpu.VMEM((256, 256), BF16))
        elif shape is None:
            scratch.append(pltpu.VMEM((512, 512), BF16))
        else:
            scratch.append(pltpu.VMEM(shape, F32))
    counts = (len(LOADS), len(NAMES), len(NAMES), 8, 8, 4, 4, 4, 4)
    scratch += [pltpu.SemaphoreType.DMA((n,)) for n in counts]
    return pl.pallas_call(
        kernel,
        out_shape=(
            pltpu.VMEM((32, 128), F32),
            pltpu.VMEM((256, 128), F32),
        ),
        in_specs=[hbm] * 6,
        out_specs=(vmem, vmem),
        scratch_shapes=scratch,
        compiler_params=pltpu.CompilerParams(
            collective_id=0, has_side_effects=True, vmem_limit_bytes=60 * 1024 * 1024
        ),
    )(band_sites, test_sites, band_factor.T, prior_factor, prior_solution, prior_covariance)


def solution(mesh):
    placed = (
        P(None, "row"),
        P(None, "col"),
        P("row", "col"),
        P("row", "col"),
        P("col", "row"),
        P("row", "col"),
    )
    return jax.shard_map(
        local,
        mesh=mesh,
        in_specs=placed,
        out_specs=(P("row", "col"), P("row", "col")),
        check_vma=False,
    )
```

```python
import jax
import jax.numpy as jnp
from jax import lax
from jax.experimental import pallas as pl
from jax.experimental.pallas import tpu as pltpu
from jax.sharding import PartitionSpec as P

length_scale = 0.3
MESH = pl.DeviceIdType.MESH
F32 = jnp.float32
BF16 = jnp.bfloat16
NZ, NY, NX = 8, 8, 4


def halves(value):
    high = value.astype(BF16)
    return high, (value - high.astype(F32)).astype(BF16)


def dot(a, b, dims):
    return lax.dot_general(a, b, (dims, ((), ())), preferred_element_type=F32)


def dot3(a, b, dims=((1,), (0,))):
    (ah, al), (bh, bl) = a, b
    return dot(ah, bh, dims) + (dot(ah, bl, dims) + dot(al, bh, dims))


def upper_inverses(blocks):
    n = 128
    i = lax.broadcasted_iota(jnp.int32, (n, n), 0)
    j = lax.broadcasted_iota(jnp.int32, (n, n), 1)
    done = []
    for u in blocks:
        inv = jnp.where(i == j, 1.0 / jnp.where(i == j, u, 1.0), 0.0)
        down = jnp.sum(inv, axis=1, keepdims=True)
        across = jnp.sum(inv, axis=0, keepdims=True)
        pair = (i // 2 == j // 2) & (i < j)
        done.append(inv - jnp.where(pair, u * down * across, 0.0))
    size = 2
    while size < n:
        part = (i // (2 * size) == j // (2 * size)) & (i // size < j // size)
        left = [halves(x) for x in done]
        mid = [dot3(x, halves(jnp.where(part, u, 0.0))) for x, u in zip(left, blocks)]
        done = [x - dot3(halves(m), xh) for x, m, xh in zip(done, mid, left)]
        size *= 2
    return done


def placed_at(value, offset):
    at = lax.broadcasted_iota(jnp.int32, (32, 128), 1)
    it = lax.broadcasted_iota(jnp.int32, (32, 128), 0)
    return lax.dot_general(
        value, (at == it + offset).astype(F32), (((1,), (0,)), ((), ())),
        precision=lax.Precision.HIGHEST, preferred_element_type=F32,
    )


NAMES = (
    "lz", "bz", "lp", "bp", "ly0", "ly1", "lx0", "lx1", "lq0", "lq1", "w",
    "a", "ap", "ts", "rx", "cy", "ux", "uy", "ry", "rz", "cp", "hy", "hx", "hg", "hf", "cd",
)
K = {name: k for k, name in enumerate(NAMES)}
LOADS = ("lf", "bs", "a", "ts", "s", "pc")
TAKING = ((2, 8), (4, 6))
BLOCKS = [(j, q) for j in range(4) for q in range(j, 4)]
NEAR_FIRST = (1, 7, 2, 6, 3, 5, 4)
FAR_FIRST = (4, 3, 5, 2, 6, 1, 7)


LAST = 3


def added(terms):
    while len(terms) > 1:
        terms = [terms[i] + terms[i + 1] for i in range(0, len(terms), 2)]
    return terms[0]


def order_of(zz):
    turn = 2 * (zz % 2) - 1
    return [(zz // 2 + o) % 4 for o in (0, 4 + turn, 4 - turn, 2)]


def kernel(
    bs_in, ts_in, lf_in, a_in, s_in, pc_in, v_out, cov_out,
    bs, ts, lf, a, s, pc,
    abuf, sh, sl, pb, xb, xs, ub, hb, hs, hx, hg, tsb, tsr, lps, bss, lzo, lzp, bzo, bzp, lt16, lt, wf, wh, wl,
    cr, own, rr, zb, rc, acc, vs,
    load, send, rec, a_rec, ap_rec, ux_rec, uy_rec, ry_rec, rz_rec, rx_rec, cy_rec, cp_rec, hy_rec, hx_rec, hg_rec, hf_rec,
):
    row = lax.axis_index("row")
    col = lax.axis_index("col")
    z, core = row // 2, row % 2
    y, x = col // NX, col % NX
    partner = (2 * z + 1 - core, col)
    takes = core == x // 2
    rests = core != x // 2
    half = x % 2
    next_x = 2 * core + 1 - half
    far_x = (x + 2) % NX
    order = order_of(z)

    def at_z(zz):
        return (2 * zz + core, col)

    def across_z(zz):
        return (2 * zz + 1 - core, col)

    def at_y(yy):
        return (row, yy * NX + x)

    def at_x(xx):
        return (row, y * NX + xx)

    def push(src, dst, name, device, recv=None):
        pltpu.make_async_remote_copy(
            src_ref=src,
            dst_ref=dst,
            send_sem=send.at[K[name]],
            recv_sem=rec.at[K[name]] if recv is None else recv,
            device_id=device,
            device_id_type=MESH,
        ).start()

    def await_bytes(ref, sem):
        pltpu.make_async_copy(ref, ref, sem).wait()

    with jax.named_scope("signals"):
        barrier = pltpu.get_barrier_semaphore()
        peers = []
        for d in FAR_FIRST:
            peers += [at_z((z + d) % NZ), at_y((y + d) % NY)]
        peers += [at_x((x + d) % NX) for d in (2, 1, 3)] + [partner]
        for peer in peers:
            pl.semaphore_signal(barrier, inc=1, device_id=peer, device_id_type=MESH)

        @pl.when(rests)
        def _():
            for d in FAR_FIRST:
                pl.semaphore_signal(barrier, inc=1, device_id=across_z((z + d) % NZ), device_id_type=MESH)

    into = dict(lf=(lf_in, lf), bs=(bs_in, bs), a=(a_in, a), ts=(ts_in, ts), s=(s_in, s), pc=(pc_in, pc))
    loads = {n: pltpu.make_async_copy(*into[n], load.at[k]) for k, n in enumerate(LOADS)}
    for n in LOADS:
        loads[n].start()

    with jax.named_scope("prepare"):
        loads["lf"].wait()
        lps[...] = placed_at(lf[0:8], 32 * core) + placed_at(lf[8:16], 64 + 32 * core)
        loads["bs"].wait()
        bss[...] = placed_at(bs[...], 32 * (row % 4))
        loads["a"].wait()

    with jax.named_scope("barrier"):
        pl.when(takes)(lambda: pl.semaphore_wait(barrier, len(peers) + NZ - 1))
        pl.when(rests)(lambda: pl.semaphore_wait(barrier, len(peers)))

    root = takes & (y == z)
    with jax.named_scope("first_sends"):
        for d in FAR_FIRST:
            push(lps, lzo.at[z], "lz", at_z((z + d) % NZ))
        push(a, abuf.at[z, core], "ap", partner, ap_rec.at[z])
        for d in NEAR_FIRST:
            push(a, abuf.at[z, core], "a", at_z((z + d) % NZ), a_rec.at[z])
        for d in FAR_FIRST:
            push(bss, bzo.at[z], "bz", at_z((z + d) % NZ))
        abuf[z, core] = a[...]
        lzo[z] = lps[...]
        bzo[z] = bss[...]
        loads["ts"].wait()

        @pl.when(root)
        def _():
            for k in range(2):
                tsb[:, k] = jnp.broadcast_to(ts[k : k + 1], (128, 128)).T.reshape(NY, 16, 128)
            for d in FAR_FIRST:
                yy = (y + d) % NY
                push(tsb.at[yy], tsr, "ts", at_y(yy))
            tsr[...] = tsb[y]

        loads["s"].wait()
        sh[...], sl[...] = halves(s[...].T)

    def pass_on(o):
        with jax.named_scope("pass_on"):
            for zz in (2 * order[o], 2 * order[o] + 1):

                @pl.when(zz != z)
                def _():
                    await_bytes(a, a_rec.at[zz])
                    push(abuf.at[zz, core], abuf.at[zz, core], "ap", partner, ap_rec.at[zz])

    def product(o):
        p = order[o]
        with jax.named_scope("a_wait"):
            for zz in (2 * p, 2 * p + 1):
                await_bytes(a, ap_rec.at[zz])
        with jax.named_scope("product"):
            rows = abuf[pl.ds(2 * p, 2)].reshape(128, 256)
            out = dot3((sh[...], sl[...]), halves(rows), ((1,), (1,)))
            pb[o] = out.reshape(2, NY, 16, 128)
            push(pb.at[o, 1 - half], xb.at[o, rests.astype(jnp.int32)], "ux", at_x(next_x), ux_rec.at[o])

            @pl.when(rests)
            def _():
                for d in FAR_FIRST:
                    yy = (y + d) % NY
                    push(pb.at[o, half, yy], hb.at[o, y], "hy", at_y(yy), hy_rec.at[o])
                hb[o, y] = pb[o, half, y]

    def helper_sum(o):
        with jax.named_scope("helper_wait"):
            await_bytes(hb.at[o, 0:7], hy_rec.at[o])
        with jax.named_scope("helper_sum"):
            hs[o] = added([hb[o, k] for k in range(NY)])
            push(hs.at[o], hx.at[o], "hx", at_x(far_x), hx_rec.at[o])

    def helper_forward(o):
        with jax.named_scope("helper_wait"):
            await_bytes(hg.at[o], hg_rec.at[o])
        with jax.named_scope("helper_forward"):
            p = order[o]
            for d in FAR_FIRST:
                push(hg.at[o], rr.at[p, half, y], "hf", at_y((y + d) % NY), hf_rec.at[o])
            rr[p, half, y] = hg[o]

    def x_sum(o):
        with jax.named_scope("x_wait"):
            await_bytes(xb.at[o], ux_rec.at[o])
        with jax.named_scope("x_sum"):
            xs[o] = (xb[o, 0] + xb[o, 1]) + pb[o, half]
            for d in FAR_FIRST:
                yy = (y + d) % NY
                push(xs.at[o, yy], ub.at[o, y], "uy", at_y(yy), uy_rec.at[o])
            ub[o, y] = xs[o, y]

    def cross():
        with jax.named_scope("cross"):

            @pl.when(y != z)
            def _():
                await_bytes(tsr, rec.at[K["ts"]])

            await_bytes(bzp, rec.at[K["bp"]])
            for p in range(4):
                spots = (bzo[2 * p] + bzp[2 * p]) + (bzo[2 * p + 1] + bzp[2 * p + 1])
                dx = tsr[0] - spots[0:1]
                dy = tsr[1] - spots[1:2]
                scaled = jnp.sqrt(dx * dx + dy * dy + 1e-06) * (3.0**0.5 / length_scale)
                cr[p] = (1.0 + scaled) * jnp.exp(-scaled)

    def y_sum(o):
        with jax.named_scope("y_wait"):
            await_bytes(ub.at[o, 0:7], uy_rec.at[o])
            await_bytes(hx.at[o], hx_rec.at[o])
        with jax.named_scope("y_sum"):
            p = order[o]
            value = cr[p] - (added([ub[o, k] for k in range(NY)]) + hx[o])
            own[o] = value
            push(own.at[o], hg.at[o], "hg", at_x(far_x), hg_rec.at[o])
            for d in FAR_FIRST:
                push(own.at[o], zb.at[o, z], "rz", at_z((z + d) % NZ), rz_rec.at[o])
                if o == LAST:
                    push(own.at[o], zb.at[o, z], "cd", across_z((z + d) % NZ), rz_rec.at[o])
            if o == LAST:
                push(own.at[o], zb.at[o, z], "cd", partner, rz_rec.at[o])
            for d in FAR_FIRST:
                push(own.at[o], rr.at[p, half, y], "ry", at_y((y + d) % NY), ry_rec.at[o])
            rr[p, half, y] = value
            zb[o, z] = value

    def to_column(o):
        with jax.named_scope("z_wait"):
            if o == LAST:
                pl.when(takes)(lambda: await_bytes(zb.at[0, 0:7], rz_rec.at[o]))
                pl.when(rests)(lambda: await_bytes(zb.at[0], rz_rec.at[o]))
            else:
                await_bytes(zb.at[0, 0:7], rz_rec.at[o])
        with jax.named_scope("to_column"):
            for zz in range(NZ):
                p = order_of(zz)[o]

                @pl.when(zz != y)
                def _():
                    push(zb.at[o, zz], rc.at[p, y], "cy", at_y(zz), cy_rec.at[o])

                @pl.when(zz == y)
                def _():
                    rc[p, y] = zb[o, zz]

    def hand_over(o):
        with jax.named_scope("hand_over"):
            await_bytes(rc.at[0, 0:7], cy_rec.at[o])
            there = rc.at[order_of(y)[o]]
            push(there, there, "cp", partner, cp_rec.at[o])

    def to_row(o):
        with jax.named_scope("r_wait"):
            await_bytes(rr.at[0, 0, 0:7], ry_rec.at[o])
        with jax.named_scope("to_row"):
            for d in (1, 3):
                there = rr.at[order[o], half]
                push(there, there, "rx", at_x((x + d) % NX), rx_rec.at[o])

    first_taking = 2 + 2 * core
    second_taking = 8 - 2 * core
    first_in = y < first_taking
    second_in = y < second_taking

    def await_some(slot, count, options, name):
        for n in options:

            @pl.when(count == n)
            def _():
                await_bytes(lt.at[0, slot, 0:n, 0], rec.at[K[name]])

    def factor_z():
        with jax.named_scope("factor_z"):
            await_bytes(lzo.at[0:7], rec.at[K["lz"]])
            push(lzo, lzp, "lp", partner)

    def sites_z():
        with jax.named_scope("sites_z"):
            await_bytes(bzo.at[0:7], rec.at[K["bz"]])
            push(bzo, bzp, "bp", partner)

    def factor_y():
        with jax.named_scope("factor_y"):
            await_bytes(lzp, rec.at[K["lp"]])
            low = lax.broadcasted_iota(jnp.int32, (8, 128), 1) < 64
            for q in range(4):
                t0, t1 = (lzo[k] + lzp[k] for k in (2 * q, 2 * q + 1))
                lt16[q, 0:8] = jnp.where(low, t0, pltpu.roll(t1, 64, 1))
                lt16[q, 8:16] = jnp.where(low, pltpu.roll(t0, 64, 1), t1)
            lt[core, 0, y, x] = lt16[core]
            lt[core, 1, y, x] = lt16[3 - core]

            def along_y(slot):
                here = lt.at[core, slot, y, x]
                for d in FAR_FIRST:
                    push(here, here, f"ly{slot}", at_y((y + d) % NY))

            pl.when(first_in)(lambda: along_y(0))
            pl.when(second_in)(lambda: along_y(1))

    def each_part(body):
        for k in range(2):

            @pl.when(core == k)
            def _():
                for slot in range(2):
                    body(k, slot, TAKING[k][slot])

    def factor_x():
        with jax.named_scope("factor_x"):
            await_some(0, first_taking - first_in.astype(jnp.int32), (1, 2, 3, 4), "ly0")
            await_some(1, second_taking - second_in.astype(jnp.int32), (5, 6, 7), "ly1")

            def along_x(k, slot, n):
                part = lt.at[k, slot, 0:n, x]
                for d in (2, 1, 3):
                    push(part, part, f"lx{slot}", at_x((x + d) % NX))

            each_part(along_x)

    def factor_arrives():
        with jax.named_scope("factor_arrives"):
            each_part(lambda k, slot, n: await_bytes(lt.at[k, slot, 0:n, 0:3], rec.at[K[f"lx{slot}"]]))

    def factor_pair():
        with jax.named_scope("factor_pair"):

            def across(k, slot, n):
                part = lt.at[k, slot, 0:n]
                push(part, part, f"lq{slot}", partner)

            each_part(across)

    def inverse(between):
        where = {0: (0, 0), 3: (0, 1), 1: (1, 0), 2: (1, 1)}

        def tile(j, q):
            k, slot = where[q]
            return lt[k, slot, 2 * j : 2 * j + 2].reshape(128, 128)

        def block(j, q):
            return halves(tile(j, q))

        with jax.named_scope("pair_wait"):
            for k in range(2):

                @pl.when(core == 1 - k)
                def _():
                    for slot in range(2):
                        await_bytes(lt.at[k, slot, 0 : TAKING[k][slot]], rec.at[K[f"lq{slot}"]])

        with jax.named_scope("diagonal"):
            w = upper_inverses([tile(q, q) for q in range(4)])
        between()
        with jax.named_scope("inverse"):
            ws = [halves(v) for v in w]
            w01 = -dot3(halves(dot3(ws[0], block(0, 1))), ws[1])
            w23 = -dot3(halves(dot3(ws[2], block(2, 3))), ws[3])
            h01, h23 = halves(w01), halves(w23)
            t02 = halves(dot3(ws[0], block(0, 2)) + dot3(h01, block(1, 2)))
            t03 = halves(dot3(ws[0], block(0, 3)) + dot3(h01, block(1, 3)))
            t12 = halves(dot3(ws[1], block(1, 2)))
            t13 = halves(dot3(ws[1], block(1, 3)))
            w02 = -dot3(t02, ws[2])
            w03 = -(dot3(t02, h23) + dot3(t03, ws[3]))
            w12 = -dot3(t12, ws[2])
            w13 = -(dot3(t12, h23) + dot3(t13, ws[3]))
            full = {(0, 0): w[0], (1, 1): w[1], (2, 2): w[2], (3, 3): w[3]}
            full.update({(0, 1): w01, (2, 3): w23, (0, 2): w02, (0, 3): w03, (1, 2): w12, (1, 3): w13})
            for k, at in enumerate(BLOCKS):
                wf[k] = full[at]
            push(wf, wf, "w", partner)

    def split_inverse():
        with jax.named_scope("split"):
            for k, (j, q) in enumerate(BLOCKS):
                here = (slice(128 * j, 128 * j + 128), slice(128 * q, 128 * q + 128))
                wh[here], wl[here] = halves(wf[k])

    with jax.named_scope("zeros"):
        for j in range(1, 4):
            for ref in (wh, wl):
                ref[128 * j : 128 * j + 128, 0 : 128 * j] = jnp.zeros((128, 128 * j), BF16)

    pass_on(0)
    factor_z()
    pass_on(1)
    product(0)
    factor_y()
    pass_on(2)
    product(1)
    pass_on(3)
    product(2)
    sites_z()
    product(3)

    @pl.when(takes)
    def _():
        x_sum(0)
        x_sum(1)
        cross()
        x_sum(2)
        factor_x()
        x_sum(3)
        y_sum(0)
        y_sum(1)
        factor_arrives()
        factor_pair()
        y_sum(2)
        y_sum(3)
        for o in range(4):
            to_column(o)
            to_row(o)
        hand_over(0)
        with jax.named_scope("inverse_wait"):
            await_bytes(wf, rec.at[K["w"]])
        hand_over(1)

    def first_two():
        helper_forward(0)
        helper_forward(1)

    @pl.when(rests)
    def _():
        helper_sum(0)
        helper_sum(1)
        factor_x()
        helper_sum(2)
        helper_sum(3)
        factor_arrives()
        inverse(first_two)
        helper_forward(2)
        helper_forward(3)
        to_column(LAST)
        await_bytes(bzp, rec.at[K["bp"]])

    split_inverse()

    def solved(chunks, rights):
        rows = [pl.ds(pl.multiple_of(128 * p, 128), 128) for p in chunks]
        solver = [jnp.concatenate([ref[at] for at in rows], axis=0) for ref in (wh, wl)]
        return dot3(halves(jnp.concatenate(rights, axis=1)), solver)

    def row_part(turns):
        with jax.named_scope("row_wait"):
            for o in turns:
                await_bytes(rr.at[0, 0], rx_rec.at[o])
                pl.when(rests)(lambda: await_bytes(rr.at[0, 0, 0:7], hf_rec.at[o]))
        with jax.named_scope("row_solve"):
            chunks = [order[o] for o in turns]
            return solved(chunks, [rr[p].reshape(256, 128) for p in chunks])

    def column_part(turns):
        with jax.named_scope("column_wait"):

            for o in turns:
                if o == LAST:
                    await_bytes(rc.at[0, 0:7], cy_rec.at[o])
                else:
                    pl.when(rests)(lambda: await_bytes(rc.at[0], cp_rec.at[o]))

        with jax.named_scope("column_solve"):
            chunks = [order_of(y)[o] for o in turns]
            return solved(chunks, [rc[p].reshape(128, 128) for p in chunks])

    acc[0:256] = row_part((0, 1, 2))
    pl.when(takes)(lambda: hand_over(2))
    acc[256:384] = column_part((0, 1, 2))
    vr = halves(acc[0:256] + row_part((3,)))
    loads["pc"].wait()
    vc = acc[256:384] + column_part((3,))
    with jax.named_scope("update"):
        cov_out[...] = pc[...] - dot3(vr, halves(vc), ((1,), (1,)))
        for p in range(4):
            vs[p] = vc[:, 128 * p : 128 * p + 128]
        vs[4] = vs[row // 4].T
        v_out[...] = vs[4, pl.ds(pl.multiple_of(32 * (row % 4), 32), 32)]

    with jax.named_scope("drain"):
        await_bytes(lzo.at[0:7], send.at[K["lz"]])
        await_bytes(bzo.at[0:7], send.at[K["bz"]])
        await_bytes(lzo, send.at[K["lp"]])
        await_bytes(bzo, send.at[K["bp"]])
        pl.when(first_in)(lambda: await_bytes(lt.at[0, 0, 0:7, 0], send.at[K["ly0"]]))
        pl.when(second_in)(lambda: await_bytes(lt.at[0, 1, 0:7, 0], send.at[K["ly1"]]))
        each_part(lambda k, slot, n: await_bytes(lt.at[k, slot, 0:n, 0:3], send.at[K[f"lx{slot}"]]))
        await_bytes(abuf.at[0:7, 0], send.at[K["a"]])
        await_bytes(abuf.at[:, 0], send.at[K["ap"]])
        await_bytes(xb.at[:, 0], send.at[K["ux"]])

        @pl.when(root)
        def _():
            await_bytes(tsb.at[0:7], send.at[K["ts"]])

        @pl.when(takes)
        def _():
            each_part(lambda k, slot, n: await_bytes(lt.at[k, slot, 0:n], send.at[K[f"lq{slot}"]]))
            await_bytes(own, send.at[K["hg"]])
            await_bytes(ub.at[:, 0:7], send.at[K["uy"]])
            await_bytes(zb.at[:, 0:7], send.at[K["rz"]])
            await_bytes(rc.at[:, 0:7], send.at[K["cy"]])
            await_bytes(rc.at[0:3], send.at[K["cp"]])
            await_bytes(zb.at[0], send.at[K["cd"]])
            await_bytes(zb.at[:, 0:7], send.at[K["ry"]])
            await_bytes(xb, send.at[K["rx"]])

        @pl.when(rests)
        def _():
            await_bytes(hb.at[:, 0:7], send.at[K["hy"]])
            await_bytes(hs, send.at[K["hx"]])
            await_bytes(rc.at[0, 0:7], send.at[K["cy"]])
            await_bytes(hb.at[:, 0:7], send.at[K["hf"]])
            await_bytes(wf, send.at[K["w"]])


def local(band_sites, test_sites, band_factor, prior_factor, prior_solution, prior_covariance):
    vmem = pl.BlockSpec(memory_space=pltpu.VMEM)
    hbm = pl.BlockSpec(memory_space=pltpu.HBM)
    arrays = [
        (2, 32), (2, 128), (16, 32), (32, 256), (256, 256), (256, 128),
        (8, 2, 32, 256),
        BF16, BF16,
        (4, 2, NY, 16, 128),
        (4, 2, NY, 16, 128),
        (4, NY, 16, 128),
        (4, NY, 16, 128),
        (4, NY, 16, 128),
        (4, 16, 128), (4, 16, 128), (4, 16, 128),
        (NY, 2, 16, 128),
        (2, 16, 128),
        (8, 128), (2, 128),
        (8, 8, 128), (8, 8, 128),
        (8, 2, 128), (8, 2, 128),
        (4, 16, 128),
        (2, 2, 8, 4, 16, 128),
        (10, 128, 128),
        None, None,
        (4, 16, 128), (4, 16, 128),
        (4, 2, NY, 16, 128),
        (4, NZ, 16, 128),
        (4, NY, 16, 128),
        (384, 512),
        (5, 128, 128),
    ]
    scratch = []
    for shape in arrays:
        if shape is BF16:
            scratch.append(pltpu.VMEM((256, 256), BF16))
        elif shape is None:
            scratch.append(pltpu.VMEM((512, 512), BF16))
        else:
            scratch.append(pltpu.VMEM(shape, F32))
    counts = (len(LOADS), len(NAMES), len(NAMES), 8, 8, *[4] * 11)
    scratch += [pltpu.SemaphoreType.DMA((n,)) for n in counts]
    return pl.pallas_call(
        kernel,
        out_shape=(
            pltpu.VMEM((32, 128), F32),
            pltpu.VMEM((256, 128), F32),
        ),
        in_specs=[hbm] * 6,
        out_specs=(vmem, vmem),
        scratch_shapes=scratch,
        compiler_params=pltpu.CompilerParams(
            collective_id=0, has_side_effects=True, vmem_limit_bytes=60 * 1024 * 1024
        ),
    )(band_sites, test_sites, band_factor.T, prior_factor, prior_solution, prior_covariance)


def solution(mesh):
    placed = (
        P(None, "row"),
        P(None, "col"),
        P("row", "col"),
        P("row", "col"),
        P("col", "row"),
        P("row", "col"),
    )
    return jax.shard_map(
        local,
        mesh=mesh,
        in_specs=placed,
        out_specs=(P("row", "col"), P("row", "col")),
        check_vma=False,
    )
```

```python
import jax
import jax.numpy as jnp
from jax import lax
from jax.experimental import pallas as pl
from jax.experimental.pallas import tpu as pltpu
from jax.sharding import PartitionSpec as P

length_scale = 0.3
MESH = pl.DeviceIdType.MESH
F32 = jnp.float32
BF16 = jnp.bfloat16
NZ, NY, NX = 8, 8, 4


def halves(value):
    high = value.astype(BF16)
    return high, (value - high.astype(F32)).astype(BF16)


def dot(a, b, dims):
    return lax.dot_general(a, b, (dims, ((), ())), preferred_element_type=F32)


def dot3(a, b, dims=((1,), (0,))):
    (ah, al), (bh, bl) = a, b
    return dot(ah, bh, dims) + (dot(ah, bl, dims) + dot(al, bh, dims))


def upper_inverses(blocks):
    n = 128
    i = lax.broadcasted_iota(jnp.int32, (n, n), 0)
    j = lax.broadcasted_iota(jnp.int32, (n, n), 1)
    done = []
    for u in blocks:
        inv = jnp.where(i == j, 1.0 / jnp.where(i == j, u, 1.0), 0.0)
        down = jnp.sum(inv, axis=1, keepdims=True)
        across = jnp.sum(inv, axis=0, keepdims=True)
        pair = (i // 2 == j // 2) & (i < j)
        done.append(inv - jnp.where(pair, u * down * across, 0.0))
    size = 2
    while size < n:
        part = (i // (2 * size) == j // (2 * size)) & (i // size < j // size)
        left = [halves(x) for x in done]
        mid = [dot3(x, halves(jnp.where(part, u, 0.0))) for x, u in zip(left, blocks)]
        done = [x - dot3(halves(m), xh) for x, m, xh in zip(done, mid, left)]
        size *= 2
    return done


def placed_at(value, offset):
    at = lax.broadcasted_iota(jnp.int32, (32, 128), 1)
    it = lax.broadcasted_iota(jnp.int32, (32, 128), 0)
    return lax.dot_general(
        value, (at == it + offset).astype(F32), (((1,), (0,)), ((), ())),
        precision=lax.Precision.HIGHEST, preferred_element_type=F32,
    )


NAMES = (
    "lz", "bz", "lp", "bp", "ly0", "ly1", "lx0", "lx1", "lq0", "lq1", "w",
    "a", "ap", "ts", "rx", "cy", "ux", "uy", "ry", "rz", "cp",
)
K = {name: k for k, name in enumerate(NAMES)}
LOADS = ("lf", "bs", "a", "ts", "s", "pc")
TAKING = ((2, 8), (4, 6))
BLOCKS = [(j, q) for j in range(4) for q in range(j, 4)]
NEAR_FIRST = (1, 7, 2, 6, 3, 5, 4)
FAR_FIRST = (4, 3, 5, 2, 6, 1, 7)


def order_of(zz):
    turn = 2 * (zz % 2) - 1
    return [(zz // 2 + o) % 4 for o in (0, 4 + turn, 4 - turn, 2)]


def kernel(
    bs_in, ts_in, lf_in, a_in, s_in, pc_in, v_out, cov_out,
    bs, ts, lf, a, s, pc,
    abuf, sh, sl, pb, xb, xs, ub, tsb, tsr, lps, bss, lzo, lzp, bzo, bzp, lt16, lt, wf, wh, wl,
    cr, own, rr, zb, rc, acc, vs,
    load, send, rec, a_rec, ap_rec, ux_rec, uy_rec, ry_rec, rz_rec, rx_rec, cy_rec, cp_rec,
):
    row = lax.axis_index("row")
    col = lax.axis_index("col")
    z, core = row // 2, row % 2
    y, x = col // NX, col % NX
    partner = (2 * z + 1 - core, col)
    takes = core == x // 2
    rests = core != x // 2
    half = x % 2
    order = order_of(z)

    def at_z(zz):
        return (2 * zz + core, col)

    def at_y(yy):
        return (row, yy * NX + x)

    def at_x(xx):
        return (row, y * NX + xx)

    def push(src, dst, name, device, recv=None):
        pltpu.make_async_remote_copy(
            src_ref=src,
            dst_ref=dst,
            send_sem=send.at[K[name]],
            recv_sem=rec.at[K[name]] if recv is None else recv,
            device_id=device,
            device_id_type=MESH,
        ).start()

    def await_bytes(ref, sem):
        pltpu.make_async_copy(ref, ref, sem).wait()

    with jax.named_scope("signals"):
        barrier = pltpu.get_barrier_semaphore()
        peers = []
        for d in FAR_FIRST:
            peers += [at_z((z + d) % NZ), at_y((y + d) % NY)]
        peers += [at_x((x + d) % NX) for d in (2, 1, 3)] + [partner]
        for peer in peers:
            pl.semaphore_signal(barrier, inc=1, device_id=peer, device_id_type=MESH)

    into = dict(lf=(lf_in, lf), bs=(bs_in, bs), a=(a_in, a), ts=(ts_in, ts), s=(s_in, s), pc=(pc_in, pc))
    loads = {n: pltpu.make_async_copy(*into[n], load.at[k]) for k, n in enumerate(LOADS)}
    for n in LOADS:
        loads[n].start()

    with jax.named_scope("prepare"):
        loads["lf"].wait()
        lps[...] = placed_at(lf[0:8], 32 * core) + placed_at(lf[8:16], 64 + 32 * core)
        loads["bs"].wait()
        bss[...] = placed_at(bs[...], 32 * (row % 4))
        loads["a"].wait()

    with jax.named_scope("barrier"):
        pl.semaphore_wait(barrier, len(peers))

    root = takes & (y == z)
    with jax.named_scope("first_sends"):
        for d in FAR_FIRST:
            push(lps, lzo.at[z], "lz", at_z((z + d) % NZ))
        push(a, abuf.at[z, core], "ap", partner, ap_rec.at[z])
        for d in NEAR_FIRST:
            push(a, abuf.at[z, core], "a", at_z((z + d) % NZ), a_rec.at[z])
        for d in FAR_FIRST:
            push(bss, bzo.at[z], "bz", at_z((z + d) % NZ))
        abuf[z, core] = a[...]
        lzo[z] = lps[...]
        bzo[z] = bss[...]
        loads["ts"].wait()

        @pl.when(root)
        def _():
            for k in range(2):
                tsb[:, k] = jnp.broadcast_to(ts[k : k + 1], (128, 128)).T.reshape(NY, 16, 128)
            for d in FAR_FIRST:
                yy = (y + d) % NY
                push(tsb.at[yy], tsr, "ts", at_y(yy))
            tsr[...] = tsb[y]

        loads["s"].wait()
        sh[...], sl[...] = halves(s[...].T)

    def pass_on(o):
        with jax.named_scope("pass_on"):
            for zz in (2 * order[o], 2 * order[o] + 1):

                @pl.when(zz != z)
                def _():
                    await_bytes(a, a_rec.at[zz])
                    push(abuf.at[zz, core], abuf.at[zz, core], "ap", partner, ap_rec.at[zz])

    def product(o):
        p = order[o]
        with jax.named_scope("a_wait"):
            for zz in (2 * p, 2 * p + 1):
                await_bytes(a, ap_rec.at[zz])
        with jax.named_scope("product"):
            rows = abuf[pl.ds(2 * p, 2)].reshape(128, 256)
            out = dot3((sh[...], sl[...]), halves(rows), ((1,), (1,)))
            pb[o] = out.reshape(2, NY, 16, 128)
            for h in range(2):
                xx = 2 * core + h

                @pl.when(xx != x)
                def _():
                    push(pb.at[o, h], xb.at[o, x], "ux", at_x(xx), ux_rec.at[o])

                @pl.when(xx == x)
                def _():
                    xb[o, x] = pb[o, h]

    def x_sum(o):
        with jax.named_scope("x_wait"):
            await_bytes(xb.at[o, 0:3], ux_rec.at[o])
        with jax.named_scope("x_sum"):
            xs[o] = (xb[o, 0] + xb[o, 1]) + (xb[o, 2] + xb[o, 3])
            for d in FAR_FIRST:
                yy = (y + d) % NY
                push(xs.at[o, yy], ub.at[o, y], "uy", at_y(yy), uy_rec.at[o])
            ub[o, y] = xs[o, y]

    def cross():
        with jax.named_scope("cross"):

            @pl.when(y != z)
            def _():
                await_bytes(tsr, rec.at[K["ts"]])

            await_bytes(bzp, rec.at[K["bp"]])
            for p in range(4):
                spots = (bzo[2 * p] + bzp[2 * p]) + (bzo[2 * p + 1] + bzp[2 * p + 1])
                dx = tsr[0] - spots[0:1]
                dy = tsr[1] - spots[1:2]
                scaled = jnp.sqrt(dx * dx + dy * dy + 1e-06) * (3.0**0.5 / length_scale)
                cr[p] = (1.0 + scaled) * jnp.exp(-scaled)

    def y_sum(o):
        with jax.named_scope("y_wait"):
            await_bytes(ub.at[o, 0:7], uy_rec.at[o])
        with jax.named_scope("y_sum"):
            p = order[o]
            terms = [ub[o, k] for k in range(NY)]
            while len(terms) > 1:
                terms = [terms[i] + terms[i + 1] for i in range(0, len(terms), 2)]
            value = cr[p] - terms[0]
            own[o] = value
            for d in FAR_FIRST:
                push(own.at[o], zb.at[o, z], "rz", at_z((z + d) % NZ), rz_rec.at[o])
            for d in FAR_FIRST:
                push(own.at[o], rr.at[p, half, y], "ry", at_y((y + d) % NY), ry_rec.at[o])
            rr[p, half, y] = value
            zb[o, z] = value

    def to_column(o):
        with jax.named_scope("z_wait"):
            await_bytes(zb.at[0, 0:7], rz_rec.at[o])
        with jax.named_scope("to_column"):
            for zz in range(NZ):
                p = order_of(zz)[o]

                @pl.when(zz != y)
                def _():
                    push(zb.at[o, zz], rc.at[p, y], "cy", at_y(zz), cy_rec.at[o])

                @pl.when(zz == y)
                def _():
                    rc[p, y] = zb[o, zz]

    def hand_over(o):
        with jax.named_scope("hand_over"):
            await_bytes(rc.at[0, 0:7], cy_rec.at[o])
            there = rc.at[order_of(y)[o]]
            push(there, there, "cp", partner, cp_rec.at[o])

    def to_row(o):
        with jax.named_scope("r_wait"):
            await_bytes(rr.at[0, 0, 0:7], ry_rec.at[o])
        with jax.named_scope("to_row"):
            for d in (2, 1, 3):
                there = rr.at[order[o], half]
                push(there, there, "rx", at_x((x + d) % NX), rx_rec.at[o])

    first_taking = 2 + 2 * core
    second_taking = 8 - 2 * core
    first_in = y < first_taking
    second_in = y < second_taking

    def await_some(slot, count, options, name):
        for n in options:

            @pl.when(count == n)
            def _():
                await_bytes(lt.at[0, slot, 0:n, 0], rec.at[K[name]])

    def factor_z():
        with jax.named_scope("factor_z"):
            await_bytes(lzo.at[0:7], rec.at[K["lz"]])
            push(lzo, lzp, "lp", partner)

    def sites_z():
        with jax.named_scope("sites_z"):
            await_bytes(bzo.at[0:7], rec.at[K["bz"]])
            push(bzo, bzp, "bp", partner)

    def factor_y():
        with jax.named_scope("factor_y"):
            await_bytes(lzp, rec.at[K["lp"]])
            low = lax.broadcasted_iota(jnp.int32, (8, 128), 1) < 64
            for q in range(4):
                t0, t1 = (lzo[k] + lzp[k] for k in (2 * q, 2 * q + 1))
                lt16[q, 0:8] = jnp.where(low, t0, pltpu.roll(t1, 64, 1))
                lt16[q, 8:16] = jnp.where(low, pltpu.roll(t0, 64, 1), t1)
            lt[core, 0, y, x] = lt16[core]
            lt[core, 1, y, x] = lt16[3 - core]

            def along_y(slot):
                here = lt.at[core, slot, y, x]
                for d in NEAR_FIRST:
                    push(here, here, f"ly{slot}", at_y((y + d) % NY))

            pl.when(first_in)(lambda: along_y(0))
            pl.when(second_in)(lambda: along_y(1))

    def each_part(body):
        for k in range(2):

            @pl.when(core == k)
            def _():
                for slot in range(2):
                    body(k, slot, TAKING[k][slot])

    def factor_x():
        with jax.named_scope("factor_x"):
            await_some(0, first_taking - first_in.astype(jnp.int32), (1, 2, 3, 4), "ly0")
            await_some(1, second_taking - second_in.astype(jnp.int32), (5, 6, 7), "ly1")

            def along_x(k, slot, n):
                part = lt.at[k, slot, 0:n, x]
                for d in (1, 3, 2):
                    push(part, part, f"lx{slot}", at_x((x + d) % NX))

            each_part(along_x)

    def factor_arrives():
        with jax.named_scope("factor_arrives"):
            each_part(lambda k, slot, n: await_bytes(lt.at[k, slot, 0:n, 0:3], rec.at[K[f"lx{slot}"]]))

    def factor_pair():
        with jax.named_scope("factor_pair"):

            def across(k, slot, n):
                part = lt.at[k, slot, 0:n]
                push(part, part, f"lq{slot}", partner)

            each_part(across)

    def inverse():
        where = {0: (0, 0), 3: (0, 1), 1: (1, 0), 2: (1, 1)}

        def tile(j, q):
            k, slot = where[q]
            return lt[k, slot, 2 * j : 2 * j + 2].reshape(128, 128)

        def block(j, q):
            return halves(tile(j, q))

        with jax.named_scope("pair_wait"):
            for k in range(2):

                @pl.when(core == 1 - k)
                def _():
                    for slot in range(2):
                        await_bytes(lt.at[k, slot, 0 : TAKING[k][slot]], rec.at[K[f"lq{slot}"]])

        with jax.named_scope("inverse"):
            w = upper_inverses([tile(q, q) for q in range(4)])
            ws = [halves(v) for v in w]
            w01 = -dot3(halves(dot3(ws[0], block(0, 1))), ws[1])
            w23 = -dot3(halves(dot3(ws[2], block(2, 3))), ws[3])
            h01, h23 = halves(w01), halves(w23)
            t02 = halves(dot3(ws[0], block(0, 2)) + dot3(h01, block(1, 2)))
            t03 = halves(dot3(ws[0], block(0, 3)) + dot3(h01, block(1, 3)))
            t12 = halves(dot3(ws[1], block(1, 2)))
            t13 = halves(dot3(ws[1], block(1, 3)))
            w02 = -dot3(t02, ws[2])
            w03 = -(dot3(t02, h23) + dot3(t03, ws[3]))
            w12 = -dot3(t12, ws[2])
            w13 = -(dot3(t12, h23) + dot3(t13, ws[3]))
            full = {(0, 0): w[0], (1, 1): w[1], (2, 2): w[2], (3, 3): w[3]}
            full.update({(0, 1): w01, (2, 3): w23, (0, 2): w02, (0, 3): w03, (1, 2): w12, (1, 3): w13})
            for k, at in enumerate(BLOCKS):
                wf[k] = full[at]
            push(wf, wf, "w", partner)

    def split_inverse():
        with jax.named_scope("split"):
            for k, (j, q) in enumerate(BLOCKS):
                here = (slice(128 * j, 128 * j + 128), slice(128 * q, 128 * q + 128))
                wh[here], wl[here] = halves(wf[k])

    with jax.named_scope("zeros"):
        for j in range(1, 4):
            for ref in (wh, wl):
                ref[128 * j : 128 * j + 128, 0 : 128 * j] = jnp.zeros((128, 128 * j), BF16)

    pass_on(0)
    pass_on(1)
    product(0)
    factor_z()
    pass_on(2)
    product(1)
    factor_y()
    pass_on(3)
    product(2)
    sites_z()
    product(3)

    @pl.when(takes)
    def _():
        x_sum(0)
        x_sum(1)
        cross()
        x_sum(2)
        x_sum(3)
        factor_x()
        for o in range(4):
            y_sum(o)
        factor_arrives()
        factor_pair()
        for o in range(4):
            to_column(o)
            to_row(o)
        for o in range(4):
            hand_over(o)
        with jax.named_scope("inverse_wait"):
            await_bytes(wf, rec.at[K["w"]])

    @pl.when(rests)
    def _():
        factor_x()
        factor_arrives()
        inverse()
        await_bytes(bzp, rec.at[K["bp"]])

    split_inverse()

    def solved(chunks, rights):
        rows = [pl.ds(pl.multiple_of(128 * p, 128), 128) for p in chunks]
        solver = [jnp.concatenate([ref[at] for at in rows], axis=0) for ref in (wh, wl)]
        return dot3(halves(jnp.concatenate(rights, axis=1)), solver)

    def row_part(turns):
        with jax.named_scope("row_wait"):
            for o in turns:
                pl.when(takes)(lambda: await_bytes(rr.at[0, 0], rx_rec.at[o]))
                pl.when(rests)(lambda: await_bytes(rr.at[0], rx_rec.at[o]))
        with jax.named_scope("row_solve"):
            chunks = [order[o] for o in turns]
            return solved(chunks, [rr[p].reshape(256, 128) for p in chunks])

    def column_part(turns):
        with jax.named_scope("column_wait"):

            @pl.when(rests)
            def _():
                for o in turns:
                    await_bytes(rc.at[0], cp_rec.at[o])

        with jax.named_scope("column_solve"):
            chunks = [order_of(y)[o] for o in turns]
            return solved(chunks, [rc[p].reshape(128, 128) for p in chunks])

    vr = halves(row_part((0, 1, 2, 3)))
    loads["pc"].wait()
    acc[...] = column_part((0, 1, 2))
    vc = acc[...] + column_part((3,))
    with jax.named_scope("update"):
        cov_out[...] = pc[...] - dot3(vr, halves(vc), ((1,), (1,)))
        for p in range(4):
            vs[p] = vc[:, 128 * p : 128 * p + 128]
        vs[4] = vs[row // 4].T
        v_out[...] = vs[4, pl.ds(pl.multiple_of(32 * (row % 4), 32), 32)]

    with jax.named_scope("drain"):
        await_bytes(lzo.at[0:7], send.at[K["lz"]])
        await_bytes(bzo.at[0:7], send.at[K["bz"]])
        await_bytes(lzo, send.at[K["lp"]])
        await_bytes(bzo, send.at[K["bp"]])
        pl.when(first_in)(lambda: await_bytes(lt.at[0, 0, 0:7, 0], send.at[K["ly0"]]))
        pl.when(second_in)(lambda: await_bytes(lt.at[0, 1, 0:7, 0], send.at[K["ly1"]]))
        each_part(lambda k, slot, n: await_bytes(lt.at[k, slot, 0:n, 0:3], send.at[K[f"lx{slot}"]]))
        await_bytes(abuf.at[0:7, 0], send.at[K["a"]])
        await_bytes(abuf.at[:, 0], send.at[K["ap"]])

        @pl.when(root)
        def _():
            await_bytes(tsb.at[0:7], send.at[K["ts"]])

        @pl.when(takes)
        def _():
            each_part(lambda k, slot, n: await_bytes(lt.at[k, slot, 0:n], send.at[K[f"lq{slot}"]]))
            await_bytes(xb.at[:, 0], send.at[K["ux"]])
            await_bytes(ub.at[:, 0:7], send.at[K["uy"]])
            await_bytes(zb.at[:, 0:7], send.at[K["rz"]])
            await_bytes(rc.at[:, 0:7], send.at[K["cy"]])
            await_bytes(rc, send.at[K["cp"]])
            await_bytes(zb.at[:, 0:7], send.at[K["ry"]])
            await_bytes(xb.at[:, 0:3], send.at[K["rx"]])

        @pl.when(rests)
        def _():
            await_bytes(xb.at[:, 0:2], send.at[K["ux"]])
            await_bytes(wf, send.at[K["w"]])


def local(band_sites, test_sites, band_factor, prior_factor, prior_solution, prior_covariance):
    vmem = pl.BlockSpec(memory_space=pltpu.VMEM)
    hbm = pl.BlockSpec(memory_space=pltpu.HBM)
    arrays = [
        (2, 32), (2, 128), (16, 32), (32, 256), (256, 256), (256, 128),
        (8, 2, 32, 256),
        BF16, BF16,
        (4, 2, NY, 16, 128),
        (4, NX, NY, 16, 128),
        (4, NY, 16, 128),
        (4, NY, 16, 128),
        (NY, 2, 16, 128),
        (2, 16, 128),
        (8, 128), (2, 128),
        (8, 8, 128), (8, 8, 128),
        (8, 2, 128), (8, 2, 128),
        (4, 16, 128),
        (2, 2, 8, 4, 16, 128),
        (10, 128, 128),
        None, None,
        (4, 16, 128), (4, 16, 128),
        (4, 2, NY, 16, 128),
        (4, NZ, 16, 128),
        (4, NY, 16, 128),
        (128, 512),
        (5, 128, 128),
    ]
    scratch = []
    for shape in arrays:
        if shape is BF16:
            scratch.append(pltpu.VMEM((256, 256), BF16))
        elif shape is None:
            scratch.append(pltpu.VMEM((512, 512), BF16))
        else:
            scratch.append(pltpu.VMEM(shape, F32))
    counts = (len(LOADS), len(NAMES), len(NAMES), 8, 8, 4, 4, 4, 4, 4, 4, 4)
    scratch += [pltpu.SemaphoreType.DMA((n,)) for n in counts]
    return pl.pallas_call(
        kernel,
        out_shape=(
            pltpu.VMEM((32, 128), F32),
            pltpu.VMEM((256, 128), F32),
        ),
        in_specs=[hbm] * 6,
        out_specs=(vmem, vmem),
        scratch_shapes=scratch,
        compiler_params=pltpu.CompilerParams(
            collective_id=0, has_side_effects=True, vmem_limit_bytes=60 * 1024 * 1024
        ),
    )(band_sites, test_sites, band_factor.T, prior_factor, prior_solution, prior_covariance)


def solution(mesh):
    placed = (
        P(None, "row"),
        P(None, "col"),
        P("row", "col"),
        P("row", "col"),
        P("col", "row"),
        P("row", "col"),
    )
    return jax.shard_map(
        local,
        mesh=mesh,
        in_specs=placed,
        out_specs=(P("row", "col"), P("row", "col")),
        check_vma=False,
    )
```

```python
import jax
import jax.numpy as jnp
from jax import lax
from jax.experimental import pallas as pl
from jax.experimental.pallas import tpu as pltpu
from jax.sharding import PartitionSpec as P

length_scale = 0.3
MESH = pl.DeviceIdType.MESH
F32 = jnp.float32
BF16 = jnp.bfloat16
NZ, NY, NX = 8, 8, 4


def halves(value):
    high = value.astype(BF16)
    return high, (value - high.astype(F32)).astype(BF16)


def dot(a, b, dims):
    return lax.dot_general(a, b, (dims, ((), ())), preferred_element_type=F32)


def dot3(a, b, dims=((1,), (0,))):
    (ah, al), (bh, bl) = a, b
    return dot(ah, bh, dims) + (dot(ah, bl, dims) + dot(al, bh, dims))


def upper_inverses(blocks):
    n = 128
    i = lax.broadcasted_iota(jnp.int32, (n, n), 0)
    j = lax.broadcasted_iota(jnp.int32, (n, n), 1)
    done = []
    for u in blocks:
        inv = jnp.where(i == j, 1.0 / jnp.where(i == j, u, 1.0), 0.0)
        down = jnp.sum(inv, axis=1, keepdims=True)
        across = jnp.sum(inv, axis=0, keepdims=True)
        pair = (i // 2 == j // 2) & (i < j)
        done.append(inv - jnp.where(pair, u * down * across, 0.0))
    size = 2
    while size < n:
        part = (i // (2 * size) == j // (2 * size)) & (i // size < j // size)
        left = [halves(x) for x in done]
        mid = [dot3(x, halves(jnp.where(part, u, 0.0))) for x, u in zip(left, blocks)]
        done = [x - dot3(halves(m), xh) for x, m, xh in zip(done, mid, left)]
        size *= 2
    return done


def placed_at(value, offset):
    at = lax.broadcasted_iota(jnp.int32, (32, 128), 1)
    it = lax.broadcasted_iota(jnp.int32, (32, 128), 0)
    return lax.dot_general(
        value, (at == it + offset).astype(F32), (((1,), (0,)), ((), ())),
        precision=lax.Precision.HIGHEST, preferred_element_type=F32,
    )


NAMES = (
    "lz", "bz", "lp", "bp", "ly0", "ly1", "lx0", "lx1", "lq0", "lq1", "w",
    "a", "ap", "ts", "rx", "cy", "ux", "uy", "ry", "rz", "cp",
)
K = {name: k for k, name in enumerate(NAMES)}
LOADS = ("lf", "bs", "a", "ts", "s", "pc")
TAKING = ((2, 8), (4, 6))
BLOCKS = [(j, q) for j in range(4) for q in range(j, 4)]
NEAR_FIRST = (1, 7, 2, 6, 3, 5, 4)
FAR_FIRST = (4, 3, 5, 2, 6, 1, 7)


def order_of(zz):
    turn = 2 * (zz % 2) - 1
    return [(zz // 2 + o) % 4 for o in (0, 4 + turn, 4 - turn, 2)]


def kernel(
    bs_in, ts_in, lf_in, a_in, s_in, pc_in, v_out, cov_out,
    bs, ts, lf, a, s, pc,
    abuf, sh, sl, pb, xb, xs, ub, tsb, tsr, lps, bss, lzo, lzp, bzo, bzp, lt16, lt, wf, wh, wl,
    cr, own, rr, zb, rc, acc, vs,
    load, send, rec, a_rec, ap_rec, ux_rec, uy_rec, ry_rec, rz_rec, rx_rec, cy_rec, cp_rec,
):
    row = lax.axis_index("row")
    col = lax.axis_index("col")
    z, core = row // 2, row % 2
    y, x = col // NX, col % NX
    partner = (2 * z + 1 - core, col)
    takes = core == x // 2
    rests = core != x // 2
    half = x % 2
    order = order_of(z)

    def at_z(zz):
        return (2 * zz + core, col)

    def at_y(yy):
        return (row, yy * NX + x)

    def at_x(xx):
        return (row, y * NX + xx)

    def push(src, dst, name, device, recv=None):
        pltpu.make_async_remote_copy(
            src_ref=src,
            dst_ref=dst,
            send_sem=send.at[K[name]],
            recv_sem=rec.at[K[name]] if recv is None else recv,
            device_id=device,
            device_id_type=MESH,
        ).start()

    def await_bytes(ref, sem):
        pltpu.make_async_copy(ref, ref, sem).wait()

    with jax.named_scope("signals"):
        barrier = pltpu.get_barrier_semaphore()
        peers = []
        for d in FAR_FIRST:
            peers += [at_z((z + d) % NZ), at_y((y + d) % NY)]
        peers += [at_x((x + d) % NX) for d in (2, 1, 3)] + [partner]
        for peer in peers:
            pl.semaphore_signal(barrier, inc=1, device_id=peer, device_id_type=MESH)

    into = dict(lf=(lf_in, lf), bs=(bs_in, bs), a=(a_in, a), ts=(ts_in, ts), s=(s_in, s), pc=(pc_in, pc))
    loads = {n: pltpu.make_async_copy(*into[n], load.at[k]) for k, n in enumerate(LOADS)}
    for n in LOADS:
        loads[n].start()

    with jax.named_scope("prepare"):
        loads["lf"].wait()
        lps[...] = placed_at(lf[0:8], 32 * core) + placed_at(lf[8:16], 64 + 32 * core)
        loads["bs"].wait()
        bss[...] = placed_at(bs[...], 32 * (row % 4))
        loads["a"].wait()

    with jax.named_scope("barrier"):
        pl.semaphore_wait(barrier, len(peers))

    root = takes & (y == z)
    with jax.named_scope("first_sends"):
        for d in FAR_FIRST:
            push(lps, lzo.at[z], "lz", at_z((z + d) % NZ))
        push(a, abuf.at[z, core], "ap", partner, ap_rec.at[z])
        for d in NEAR_FIRST:
            push(a, abuf.at[z, core], "a", at_z((z + d) % NZ), a_rec.at[z])
        for d in FAR_FIRST:
            push(bss, bzo.at[z], "bz", at_z((z + d) % NZ))
        abuf[z, core] = a[...]
        lzo[z] = lps[...]
        bzo[z] = bss[...]
        loads["ts"].wait()

        @pl.when(root)
        def _():
            for k in range(2):
                tsb[:, k] = jnp.broadcast_to(ts[k : k + 1], (128, 128)).T.reshape(NY, 16, 128)
            for d in FAR_FIRST:
                yy = (y + d) % NY
                push(tsb.at[yy], tsr, "ts", at_y(yy))
            tsr[...] = tsb[y]

        loads["s"].wait()
        sh[...], sl[...] = halves(s[...].T)

    def pass_on(o):
        with jax.named_scope("pass_on"):
            for zz in (2 * order[o], 2 * order[o] + 1):

                @pl.when(zz != z)
                def _():
                    await_bytes(a, a_rec.at[zz])
                    push(abuf.at[zz, core], abuf.at[zz, core], "ap", partner, ap_rec.at[zz])

    def product(o):
        p = order[o]
        with jax.named_scope("a_wait"):
            for zz in (2 * p, 2 * p + 1):
                await_bytes(a, ap_rec.at[zz])
        with jax.named_scope("product"):
            rows = abuf[pl.ds(2 * p, 2)].reshape(128, 256)
            out = dot3((sh[...], sl[...]), halves(rows), ((1,), (1,)))
            pb[o] = out.reshape(2, NY, 16, 128)
            for h in range(2):
                xx = 2 * core + h

                @pl.when(xx != x)
                def _():
                    push(pb.at[o, h], xb.at[o, x], "ux", at_x(xx), ux_rec.at[o])

                @pl.when(xx == x)
                def _():
                    xb[o, x] = pb[o, h]

    def x_sum(o):
        with jax.named_scope("x_wait"):
            await_bytes(xb.at[o, 0:3], ux_rec.at[o])
        with jax.named_scope("x_sum"):
            xs[o] = (xb[o, 0] + xb[o, 1]) + (xb[o, 2] + xb[o, 3])
            for d in FAR_FIRST:
                yy = (y + d) % NY
                push(xs.at[o, yy], ub.at[o, y], "uy", at_y(yy), uy_rec.at[o])
            ub[o, y] = xs[o, y]

    def cross():
        with jax.named_scope("cross"):

            @pl.when(y != z)
            def _():
                await_bytes(tsr, rec.at[K["ts"]])

            await_bytes(bzp, rec.at[K["bp"]])
            for p in range(4):
                spots = (bzo[2 * p] + bzp[2 * p]) + (bzo[2 * p + 1] + bzp[2 * p + 1])
                dx = tsr[0] - spots[0:1]
                dy = tsr[1] - spots[1:2]
                scaled = jnp.sqrt(dx * dx + dy * dy + 1e-06) * (3.0**0.5 / length_scale)
                cr[p] = (1.0 + scaled) * jnp.exp(-scaled)

    def y_sum(o):
        with jax.named_scope("y_wait"):
            await_bytes(ub.at[o, 0:7], uy_rec.at[o])
        with jax.named_scope("y_sum"):
            p = order[o]
            terms = [ub[o, k] for k in range(NY)]
            while len(terms) > 1:
                terms = [terms[i] + terms[i + 1] for i in range(0, len(terms), 2)]
            value = cr[p] - terms[0]
            own[o] = value
            for d in FAR_FIRST:
                push(own.at[o], zb.at[o, z], "rz", at_z((z + d) % NZ), rz_rec.at[o])
            for d in FAR_FIRST:
                push(own.at[o], rr.at[p, half, y], "ry", at_y((y + d) % NY), ry_rec.at[o])
            rr[p, half, y] = value
            zb[o, z] = value

    def to_column(o):
        with jax.named_scope("z_wait"):
            await_bytes(zb.at[0, 0:7], rz_rec.at[o])
        with jax.named_scope("to_column"):
            for zz in range(NZ):
                p = order_of(zz)[o]

                @pl.when(zz != y)
                def _():
                    push(zb.at[o, zz], rc.at[p, y], "cy", at_y(zz), cy_rec.at[o])

                @pl.when(zz == y)
                def _():
                    rc[p, y] = zb[o, zz]

    def hand_over(o):
        with jax.named_scope("hand_over"):
            await_bytes(rc.at[0, 0:7], cy_rec.at[o])
            there = rc.at[order_of(y)[o]]
            push(there, there, "cp", partner, cp_rec.at[o])

    def to_row(o):
        with jax.named_scope("r_wait"):
            await_bytes(rr.at[0, 0, 0:7], ry_rec.at[o])
        with jax.named_scope("to_row"):
            for d in (2, 1, 3):
                there = rr.at[order[o], half]
                push(there, there, "rx", at_x((x + d) % NX), rx_rec.at[o])

    first_taking = 2 + 2 * core
    second_taking = 8 - 2 * core
    first_in = y < first_taking
    second_in = y < second_taking

    def await_some(slot, count, options, name):
        for n in options:

            @pl.when(count == n)
            def _():
                await_bytes(lt.at[0, slot, 0:n, 0], rec.at[K[name]])

    def factor_z():
        with jax.named_scope("factor_z"):
            await_bytes(lzo.at[0:7], rec.at[K["lz"]])
            push(lzo, lzp, "lp", partner)

    def sites_z():
        with jax.named_scope("sites_z"):
            await_bytes(bzo.at[0:7], rec.at[K["bz"]])
            push(bzo, bzp, "bp", partner)

    def factor_y():
        with jax.named_scope("factor_y"):
            await_bytes(lzp, rec.at[K["lp"]])
            low = lax.broadcasted_iota(jnp.int32, (8, 128), 1) < 64
            for q in range(4):
                t0, t1 = (lzo[k] + lzp[k] for k in (2 * q, 2 * q + 1))
                lt16[q, 0:8] = jnp.where(low, t0, pltpu.roll(t1, 64, 1))
                lt16[q, 8:16] = jnp.where(low, pltpu.roll(t0, 64, 1), t1)
            lt[core, 0, y, x] = lt16[core]
            lt[core, 1, y, x] = lt16[3 - core]

            def along_y(slot):
                here = lt.at[core, slot, y, x]
                for d in NEAR_FIRST:
                    push(here, here, f"ly{slot}", at_y((y + d) % NY))

            pl.when(first_in)(lambda: along_y(0))
            pl.when(second_in)(lambda: along_y(1))

    def each_part(body):
        for k in range(2):

            @pl.when(core == k)
            def _():
                for slot in range(2):
                    body(k, slot, TAKING[k][slot])

    def factor_x():
        with jax.named_scope("factor_x"):
            await_some(0, first_taking - first_in.astype(jnp.int32), (1, 2, 3, 4), "ly0")
            await_some(1, second_taking - second_in.astype(jnp.int32), (5, 6, 7), "ly1")

            def along_x(k, slot, n):
                part = lt.at[k, slot, 0:n, x]
                for d in (1, 3, 2):
                    push(part, part, f"lx{slot}", at_x((x + d) % NX))

            each_part(along_x)

    def factor_arrives():
        with jax.named_scope("factor_arrives"):
            each_part(lambda k, slot, n: await_bytes(lt.at[k, slot, 0:n, 0:3], rec.at[K[f"lx{slot}"]]))

    def factor_pair():
        with jax.named_scope("factor_pair"):

            def across(k, slot, n):
                part = lt.at[k, slot, 0:n]
                push(part, part, f"lq{slot}", partner)

            each_part(across)

    def inverse():
        where = {0: (0, 0), 3: (0, 1), 1: (1, 0), 2: (1, 1)}

        def tile(j, q):
            k, slot = where[q]
            return lt[k, slot, 2 * j : 2 * j + 2].reshape(128, 128)

        def block(j, q):
            return halves(tile(j, q))

        with jax.named_scope("pair_wait"):
            for k in range(2):

                @pl.when(core == 1 - k)
                def _():
                    for slot in range(2):
                        await_bytes(lt.at[k, slot, 0 : TAKING[k][slot]], rec.at[K[f"lq{slot}"]])

        with jax.named_scope("inverse"):
            w = upper_inverses([tile(q, q) for q in range(4)])
            ws = [halves(v) for v in w]
            w01 = -dot3(halves(dot3(ws[0], block(0, 1))), ws[1])
            w23 = -dot3(halves(dot3(ws[2], block(2, 3))), ws[3])
            h01, h23 = halves(w01), halves(w23)
            t02 = halves(dot3(ws[0], block(0, 2)) + dot3(h01, block(1, 2)))
            t03 = halves(dot3(ws[0], block(0, 3)) + dot3(h01, block(1, 3)))
            t12 = halves(dot3(ws[1], block(1, 2)))
            t13 = halves(dot3(ws[1], block(1, 3)))
            w02 = -dot3(t02, ws[2])
            w03 = -(dot3(t02, h23) + dot3(t03, ws[3]))
            w12 = -dot3(t12, ws[2])
            w13 = -(dot3(t12, h23) + dot3(t13, ws[3]))
            full = {(0, 0): w[0], (1, 1): w[1], (2, 2): w[2], (3, 3): w[3]}
            full.update({(0, 1): w01, (2, 3): w23, (0, 2): w02, (0, 3): w03, (1, 2): w12, (1, 3): w13})
            for k, at in enumerate(BLOCKS):
                wf[k] = full[at]
            push(wf, wf, "w", partner)

    def split_inverse():
        with jax.named_scope("split"):
            for k, (j, q) in enumerate(BLOCKS):
                here = (slice(128 * j, 128 * j + 128), slice(128 * q, 128 * q + 128))
                wh[here], wl[here] = halves(wf[k])

    with jax.named_scope("zeros"):
        for j in range(1, 4):
            for ref in (wh, wl):
                ref[128 * j : 128 * j + 128, 0 : 128 * j] = jnp.zeros((128, 128 * j), BF16)

    pass_on(0)
    pass_on(1)
    product(0)
    factor_z()
    pass_on(2)
    product(1)
    factor_y()
    pass_on(3)
    product(2)
    sites_z()
    product(3)

    @pl.when(takes)
    def _():
        x_sum(0)
        x_sum(1)
        cross()
        x_sum(2)
        x_sum(3)
        factor_x()
        for o in range(4):
            y_sum(o)
        to_column(0)
        to_row(0)
        factor_arrives()
        factor_pair()
        for o in range(1, 4):
            to_column(o)
            to_row(o)
        for o in range(4):
            hand_over(o)
        with jax.named_scope("inverse_wait"):
            await_bytes(wf, rec.at[K["w"]])

    @pl.when(rests)
    def _():
        factor_x()
        factor_arrives()
        inverse()
        await_bytes(bzp, rec.at[K["bp"]])

    split_inverse()

    def solved(chunks, rights):
        rows = [pl.ds(pl.multiple_of(128 * p, 128), 128) for p in chunks]
        solver = [jnp.concatenate([ref[at] for at in rows], axis=0) for ref in (wh, wl)]
        return dot3(halves(jnp.concatenate(rights, axis=1)), solver)

    def row_part(turns):
        with jax.named_scope("row_wait"):
            for o in turns:
                pl.when(takes)(lambda: await_bytes(rr.at[0, 0], rx_rec.at[o]))
                pl.when(rests)(lambda: await_bytes(rr.at[0], rx_rec.at[o]))
        with jax.named_scope("row_solve"):
            chunks = [order[o] for o in turns]
            return solved(chunks, [rr[p].reshape(256, 128) for p in chunks])

    def column_part(turns):
        with jax.named_scope("column_wait"):

            @pl.when(rests)
            def _():
                for o in turns:
                    await_bytes(rc.at[0], cp_rec.at[o])

        with jax.named_scope("column_solve"):
            chunks = [order_of(y)[o] for o in turns]
            return solved(chunks, [rc[p].reshape(128, 128) for p in chunks])

    vr = halves(row_part((0, 1, 2, 3)))
    loads["pc"].wait()
    acc[...] = column_part((0, 1, 2))
    vc = acc[...] + column_part((3,))
    with jax.named_scope("update"):
        cov_out[...] = pc[...] - dot3(vr, halves(vc), ((1,), (1,)))
        for p in range(4):
            vs[p] = vc[:, 128 * p : 128 * p + 128]
        vs[4] = vs[row // 4].T
        v_out[...] = vs[4, pl.ds(pl.multiple_of(32 * (row % 4), 32), 32)]

    with jax.named_scope("drain"):
        await_bytes(lzo.at[0:7], send.at[K["lz"]])
        await_bytes(bzo.at[0:7], send.at[K["bz"]])
        await_bytes(lzo, send.at[K["lp"]])
        await_bytes(bzo, send.at[K["bp"]])
        pl.when(first_in)(lambda: await_bytes(lt.at[0, 0, 0:7, 0], send.at[K["ly0"]]))
        pl.when(second_in)(lambda: await_bytes(lt.at[0, 1, 0:7, 0], send.at[K["ly1"]]))
        each_part(lambda k, slot, n: await_bytes(lt.at[k, slot, 0:n, 0:3], send.at[K[f"lx{slot}"]]))
        await_bytes(abuf.at[0:7, 0], send.at[K["a"]])
        await_bytes(abuf.at[:, 0], send.at[K["ap"]])

        @pl.when(root)
        def _():
            await_bytes(tsb.at[0:7], send.at[K["ts"]])

        @pl.when(takes)
        def _():
            each_part(lambda k, slot, n: await_bytes(lt.at[k, slot, 0:n], send.at[K[f"lq{slot}"]]))
            await_bytes(xb.at[:, 0], send.at[K["ux"]])
            await_bytes(ub.at[:, 0:7], send.at[K["uy"]])
            await_bytes(zb.at[:, 0:7], send.at[K["rz"]])
            await_bytes(rc.at[:, 0:7], send.at[K["cy"]])
            await_bytes(rc, send.at[K["cp"]])
            await_bytes(zb.at[:, 0:7], send.at[K["ry"]])
            await_bytes(xb.at[:, 0:3], send.at[K["rx"]])

        @pl.when(rests)
        def _():
            await_bytes(xb.at[:, 0:2], send.at[K["ux"]])
            await_bytes(wf, send.at[K["w"]])


def local(band_sites, test_sites, band_factor, prior_factor, prior_solution, prior_covariance):
    vmem = pl.BlockSpec(memory_space=pltpu.VMEM)
    hbm = pl.BlockSpec(memory_space=pltpu.HBM)
    arrays = [
        (2, 32), (2, 128), (16, 32), (32, 256), (256, 256), (256, 128),
        (8, 2, 32, 256),
        BF16, BF16,
        (4, 2, NY, 16, 128),
        (4, NX, NY, 16, 128),
        (4, NY, 16, 128),
        (4, NY, 16, 128),
        (NY, 2, 16, 128),
        (2, 16, 128),
        (8, 128), (2, 128),
        (8, 8, 128), (8, 8, 128),
        (8, 2, 128), (8, 2, 128),
        (4, 16, 128),
        (2, 2, 8, 4, 16, 128),
        (10, 128, 128),
        None, None,
        (4, 16, 128), (4, 16, 128),
        (4, 2, NY, 16, 128),
        (4, NZ, 16, 128),
        (4, NY, 16, 128),
        (128, 512),
        (5, 128, 128),
    ]
    scratch = []
    for shape in arrays:
        if shape is BF16:
            scratch.append(pltpu.VMEM((256, 256), BF16))
        elif shape is None:
            scratch.append(pltpu.VMEM((512, 512), BF16))
        else:
            scratch.append(pltpu.VMEM(shape, F32))
    counts = (len(LOADS), len(NAMES), len(NAMES), 8, 8, 4, 4, 4, 4, 4, 4, 4)
    scratch += [pltpu.SemaphoreType.DMA((n,)) for n in counts]
    return pl.pallas_call(
        kernel,
        out_shape=(
            pltpu.VMEM((32, 128), F32),
            pltpu.VMEM((256, 128), F32),
        ),
        in_specs=[hbm] * 6,
        out_specs=(vmem, vmem),
        scratch_shapes=scratch,
        compiler_params=pltpu.CompilerParams(
            collective_id=0, has_side_effects=True, vmem_limit_bytes=60 * 1024 * 1024
        ),
    )(band_sites, test_sites, band_factor.T, prior_factor, prior_solution, prior_covariance)


def solution(mesh):
    placed = (
        P(None, "row"),
        P(None, "col"),
        P("row", "col"),
        P("row", "col"),
        P("col", "row"),
        P("row", "col"),
    )
    return jax.shard_map(
        local,
        mesh=mesh,
        in_specs=placed,
        out_specs=(P("row", "col"), P("row", "col")),
        check_vma=False,
    )
```
